32 devices in a mesh: theta: 4 (over y, core), phi: 8 (over z, x).
Axes of the slice: x: 2, y: 2, z: 4, core: 2. Of those that a mesh axis runs over, the one named last changes fastest.
Arguments:
- density: float32 [2, 32, 768, 128], P(None, 'theta', 'phi'), may hold values from 0.5 to 2
- velocity: float32 [3, 32, 768, 128], P(None, 'theta', 'phi'), may hold values from -3 to 3
- bfield: float32 [3, 32, 768, 128], P(None, 'theta', 'phi'), may hold values from -6 to 6
- levels: int32 [2, 4], replicated, may hold values from 0 to 3
Outputs:
- density_new: float32 [2, 32, 768, 128], P(None, 'theta', 'phi')
- bfield_new: float32 [3, 32, 768, 128], P(None, 'theta', 'phi')
The draws below stay inside these ranges and needn't reach their ends.
Inputs may be any that keep to these rules, and one draw needn't show every extreme that they name: `levels`: a row at level l keeps the azimuthal modes below 128 // 2**l.
All inputs are finite; a program needn't handle non-finite values.
Results may differ from the reference program's by a relative error of at most 0.00007.
Values sent between devices are 32-bit elements; how exact they have to be, the bound alone decides.
A program may use at most 64 MiB of HBM per device.

```python
import jax
import jax.numpy as jnp
from jax import lax

NR = 128
CT = 8
CAP = 4
KMAX = 128
LEVELS = 4
NTH = 32
NPH = 768
N_THETA = 4


def touch_ends(values, own_key, least, high):
    spot = [jax.random.randint(jax.random.fold_in(own_key, axis), (), 0, length) for axis, length in enumerate(values.shape)]
    main_axis = values.shape.index(max(values.shape))
    next_to = spot[:main_axis] + [(spot[main_axis] + 1) % values.shape[main_axis]] + spot[main_axis + 1:]
    return values.at[tuple(spot)].set(least).at[tuple(next_to)].set(high)


def block_scale(stream_key, shape, shards, least, high):
    factor_of = 1.0
    for axis_at, blocks in shards:
        draws = jax.random.uniform(jax.random.fold_in(jax.random.fold_in(stream_key, 6), axis_at), (blocks,), jnp.float32, least / len(shards), high / len(shards))
        factor_of = factor_of * jnp.repeat(jnp.exp(draws), shape[axis_at] // blocks).reshape((-1,) + (1,) * (len(shape) - 1 - axis_at))
    return factor_of


def scatter_about(key, shape, scale, most, pieces=(), kind=jnp.bfloat16):
    values = scale * jax.random.normal(key, shape, jnp.float32)
    if pieces:
        values = values * block_scale(key, shape, pieces, -0.22, 0.18)
    return jnp.clip(values, -most, most).astype(kind)


def setup_inputs(seed: int = 0) -> dict:
    seeds = jax.random.split(jax.random.key(seed), 5)
    density = jnp.clip(0.5 + 1.5 * jax.random.uniform(seeds[0], (2, NTH, NPH, NR), jnp.float32) ** block_scale(seeds[0], (2, NTH, NPH, NR), ((1, 4), (2, 8)), -0.2, 0.2), 0.5, 2.0)
    velocity = scatter_about(seeds[1], (3, NTH, NPH, NR), 0.5, 3.0, ((1, 4), (2, 8)), jnp.float32)
    bfield = scatter_about(seeds[2], (3, NTH, NPH, NR), 1.0, 6.0, ((1, 4), (2, 8)), jnp.float32)
    levels = touch_ends(jax.random.randint(seeds[3], (2, CAP), 0, LEVELS), jax.random.fold_in(seeds[3], 1), 0, LEVELS - 1).astype(jnp.int32)
    return {"density": density, "velocity": velocity, "bfield": bfield, "levels": levels}


TIME_STEP = 0.2
PARITY = (1.0, 1.0, 1.0, -1.0, -1.0, 1.0, -1.0, -1.0)


def window_of(array, spans):
    return array[spans[0][0]:spans[0][1], spans[1][0]:spans[1][1], spans[2][0]:spans[2][1]]


def moved(spans, direction, start, length):
    return tuple((start, start + length) if other == direction else spans[other] for other in range(3))


def corner_mean(field, extents, first_axis, second_axis):
    base = [(1, extents[0] + 1), (1, extents[1] + 1), (1, extents[2] + 1)]
    total = jnp.zeros((), jnp.float32)
    for first_start in (0, 1):
        for second_start in (0, 1):
            spans_now = list(base)
            spans_now[first_axis] = (first_start, first_start + extents[first_axis] + 1)
            spans_now[second_axis] = (second_start, second_start + extents[second_axis] + 1)
            total = total + window_of(field, spans_now)
    return 0.25 * total


def advance(extended):
    extents = (extended.shape[1] - 4, extended.shape[2] - 4, extended.shape[3] - 4)
    inner_span = tuple((2, extent + 2) for extent in extents)
    speed_for = (3, 4, 2)
    densities = []
    for channel in range(2):
        amount = extended[channel]
        tendency = jnp.zeros(extents, jnp.float32)
        for direction in range(3):
            extent_now = extents[direction]
            lower_span = moved(inner_span, direction, 1, extent_now + 1)
            upper_span = moved(inner_span, direction, 2, extent_now + 1)
            speed_field = extended[speed_for[direction]]
            left_amount = window_of(amount, lower_span)
            right_amount = window_of(amount, upper_span)
            left_speed = window_of(speed_field, lower_span)
            right_speed = window_of(speed_field, upper_span)
            fluxes = 0.5 * (left_amount * left_speed + right_amount * right_speed) - 0.5 * jnp.maximum(jnp.abs(left_speed), jnp.abs(right_speed)) * (right_amount - left_amount)
            tendency = tendency + lax.slice_in_dim(fluxes, 1, extent_now + 1, axis=direction) - lax.slice_in_dim(fluxes, 0, extent_now, axis=direction)
        densities.append(window_of(amount, inner_span) - TIME_STEP * tendency)
    wide_span = tuple((1, extent + 3) for extent in extents)
    axis_of = (2, 0, 1)
    centred = []
    for component in range(3):
        direction = axis_of[component]
        shifted = moved(wide_span, direction, 2, extents[direction] + 2)
        face_field = extended[5 + component]
        centred.append(0.5 * (window_of(face_field, wide_span) + window_of(face_field, shifted)))
    speeds = [window_of(extended[2 + component], wide_span) for component in range(3)]
    emf_radial = -(speeds[1] * centred[2] - speeds[2] * centred[1])
    emf_theta = -(speeds[2] * centred[0] - speeds[0] * centred[2])
    emf_phi = -(speeds[0] * centred[1] - speeds[1] * centred[0])
    edge_phi = corner_mean(emf_phi, extents, 0, 2)
    edge_theta = corner_mean(emf_theta, extents, 1, 2)
    edge_radial = corner_mean(emf_radial, extents, 0, 1)
    radial_len = extents[2]
    inner_faces = [window_of(extended[5 + component], inner_span) for component in range(3)]
    new_radial = inner_faces[0] - TIME_STEP * ((edge_phi[1:, :, :radial_len] - edge_phi[:-1, :, :radial_len]) - (edge_theta[:, 1:, :radial_len] - edge_theta[:, :-1, :radial_len]))
    new_theta = inner_faces[1] - TIME_STEP * ((edge_radial[:-1, 1:, :] - edge_radial[:-1, :-1, :]) - (edge_phi[:-1, :, 1:] - edge_phi[:-1, :, :-1]))
    new_phi = inner_faces[2] - TIME_STEP * ((edge_theta[:, :-1, 1:] - edge_theta[:, :-1, :-1]) - (edge_radial[1:, :-1, :] - edge_radial[:-1, :-1, :]))
    return jnp.stack(densities), jnp.stack([new_radial, new_theta, new_phi])


def pole_filter(rows, level_row):
    spectrum = jnp.fft.rfft(rows, axis=2)
    limits = jnp.right_shift(jnp.int32(KMAX), level_row.astype(jnp.int32))
    orders = jnp.arange(spectrum.shape[2], dtype=jnp.int32)
    kept = orders[None, :] < limits[:, None]
    spectrum = jnp.where(kept[None, :, :, None], spectrum, jnp.zeros_like(spectrum))
    return jnp.fft.irfft(spectrum, n=rows.shape[2], axis=2).astype(jnp.float32)


def reference(density, velocity, bfield, levels):
    combined = jnp.concatenate([density, velocity, bfield], axis=0)
    theta_len = combined.shape[1]
    half_turn = combined.shape[2] // 2
    north_rows = pole_filter(combined[:, :CAP], levels[0])
    south_rows = pole_filter(combined[:, theta_len - CAP:], levels[1])
    combined = jnp.concatenate([north_rows, combined[:, CAP:theta_len - CAP], south_rows], axis=1)
    parity = jnp.array(PARITY, jnp.float32)[:, None, None]

    def across_pole(row_index):
        return parity * jnp.roll(combined[:, row_index], half_turn, axis=1)

    north_ghosts = jnp.stack([across_pole(1), across_pole(0)], axis=1)
    south_ghosts = jnp.stack([across_pole(theta_len - 1), across_pole(theta_len - 2)], axis=1)
    full_rows = jnp.concatenate([north_ghosts, combined, south_ghosts], axis=1)
    density_parts = []
    field_parts = []
    for block_index in range(N_THETA):
        block_rows = full_rows[:, block_index * CT:block_index * CT + CT + 4]
        block_rows = jnp.concatenate([block_rows[:, :, -2:], block_rows, block_rows[:, :, :2]], axis=2)
        block_rows = jnp.pad(block_rows, ((0, 0), (0, 0), (0, 0), (2, 2)), mode="edge")
        density_block, field_block = advance(block_rows)
        density_parts.append(density_block)
        field_parts.append(field_block)
    return jnp.concatenate(density_parts, axis=1), jnp.concatenate(field_parts, axis=1)
```

```python
import functools
import math

import jax
import jax.numpy as jnp
import numpy as np
import ml_dtypes
from jax import lax
from jax.experimental import pallas as pl
from jax.experimental.pallas import tpu as pltpu
from jax.sharding import PartitionSpec as P

CAP = 4
KMAX = 128
TIME_STEP = 0.2
CHANNELS = 8
ODD = (3, 4, 6, 7)
BTHETA = 6
BPHI = 7
MESH = pl.DeviceIdType.MESH


def split_table(table):
    high = table.astype(ml_dtypes.bfloat16)
    low = (table - high.astype(np.float64)).astype(ml_dtypes.bfloat16)
    return np.stack([high, low])


def tables(count, cols):
    cycle = count * cols
    orders = np.arange(KMAX)
    points = np.arange(cycle)
    angle = (orders[:, None] * points[None, :] % cycle) * (2.0 * math.pi / cycle)
    forward = np.concatenate([np.cos(angle), np.sin(angle)], axis=0)
    offset = np.concatenate([np.arange(cols + 7), [-1]])
    place = ((np.arange(count)[:, None] * cols + offset[None, :]) % cycle).reshape(-1)
    back = forward.T[place]
    return split_table(forward), split_table(back)


def flux(ql, qr, vl, vr):
    return 0.5 * (ql * vl + qr * vr) - 0.5 * jnp.maximum(jnp.abs(vl), jnp.abs(vr)) * (qr - ql)


def stencil_row(ext, dout, bout, row, rows, cols):
    wide = cols + 8
    lower = jnp.where(row == 0, rows + 2, row - 1)
    upper = row + 1
    upper2 = row + 2
    lane = lax.broadcasted_iota(jnp.int32, (wide, 128), 1)
    first = lane == 0
    last = lane == 127

    def from_left(x):
        return pltpu.roll(x, 1, 0)

    def from_right(x):
        return pltpu.roll(x, wide - 1, 0)

    def from_below(x):
        return pltpu.roll(x, 1, 1)

    def from_above(x):
        return pltpu.roll(x, 127, 1)

    vr, vt, vp = ext[2, row], ext[3, row], ext[4, row]
    vt_lo, vt_up = ext[3, lower], ext[3, upper]
    vp_l = from_left(vp)
    vr_b = jnp.where(first, vr, from_below(vr))
    for c in range(2):
        q = ext[c, row]
        tend = flux(q, ext[c, upper], vt, vt_up) - flux(ext[c, lower], q, vt_lo, vt)
        fp = flux(from_left(q), q, vp_l, vp)
        tend = tend + from_right(fp) - fp
        fr = flux(jnp.where(first, q, from_below(q)), q, vr_b, vr)
        tend = tend + jnp.where(last, q * vr, from_above(fr)) - fr
        new = q - TIME_STEP * tend
        dout[c, row] = new[:cols]

    def emfs(j, bt_next):
        ur, ut, up = ext[2, j], ext[3, j], ext[4, j]
        br, bt, bp = ext[5, j], ext[6, j], ext[7, j]
        br_c = 0.5 * (br + jnp.where(last, br, from_above(br)))
        bt_c = 0.5 * (bt + bt_next)
        bp_c = 0.5 * (bp + from_right(bp))
        e_r = -(ut * bp_c - up * bt_c)
        e_p = -(ur * bt_c - ut * br_c)
        e_p0 = -(ur * bt_c - ut * br)
        pair_p = e_p + jnp.where(first, e_p0, from_below(e_p))
        pair_r = e_r + from_left(e_r)
        return e_p, pair_p, pair_r, br_c, bp_c

    bt = ext[6, row]
    bt_up = ext[6, upper]
    ep_lo, pp_lo, pr_lo, _, _ = emfs(lower, bt)
    ep, pp, pr, br_c, bp_c = emfs(row, bt_up)
    ep_up, pp_up, pr_up, _, _ = emfs(upper, ext[6, upper2])
    br = ext[5, row]
    e_t = -(vp * br_c - vr * bp_c)
    e_t0 = -(vp * br - vr * bp_c)
    et_pair = e_t + from_left(e_t)
    et_pair0 = e_t0 + from_left(e_t0)
    edge_t = et_pair + jnp.where(first, et_pair0, from_below(et_pair))
    edge_t_above = jnp.where(last, 2.0 * et_pair, from_above(edge_t))
    edge_p = pp_lo + pp
    edge_p_above = jnp.where(last, 2.0 * (ep_lo + ep), from_above(edge_p))
    edge_r = pr_lo + pr
    scale = TIME_STEP * 0.25
    new_r = br - scale * ((pp_up - pp_lo) - (from_right(edge_t) - edge_t))
    new_t = bt - scale * ((from_right(edge_r) - edge_r) - (edge_p_above - edge_p))
    new_p = ext[7, row] - scale * ((edge_t_above - edge_t) - (pr_up - pr_lo))
    bout[0, row] = new_r[:cols]
    bout[1, row] = new_t[:cols]
    bout[2, row] = new_p[:cols]


def split(x):
    high = x.astype(jnp.bfloat16)
    return high, (x - high.astype(jnp.float32)).astype(jnp.bfloat16)


def product(table, x):
    high, low = split(x)
    dot = functools.partial(jnp.dot, preferred_element_type=jnp.float32)
    return dot(table[0], high) + (dot(table[0], low) + dot(table[1], high))


def kernel(
    n, nt, rows, cols,
    density, velocity, bfield, levels, fwd_hbm, back_hbm,
    dout, bout,
    ext, cyc, fil, caps, fwd, back, to_right, to_left, at_left, at_right,
    load_sem, fs, fr, rs, rr, gs, gr, g2s, g2r, hs, hr, ts, tr,
):
    per = CHANNELS * CAP // n
    groups = per // 2
    wide = cols + 8
    cycle = n * cols
    t = lax.axis_index("theta")
    me = lax.axis_index("phi")
    north = t == 0
    south = t == nt - 1
    end = north | south
    cap0 = jnp.where(north, 0, rows - CAP)
    main = pl.ds(0, cols)

    loads = [
        pltpu.make_async_copy(density, ext.at[pl.ds(0, 2), pl.ds(0, rows), main], load_sem.at[0]),
        pltpu.make_async_copy(velocity, ext.at[pl.ds(2, 3), pl.ds(0, rows), main], load_sem.at[1]),
        pltpu.make_async_copy(bfield, ext.at[pl.ds(5, 3), pl.ds(0, rows), main], load_sem.at[2]),
    ]
    table_loads = [
        pltpu.make_async_copy(fwd_hbm, fwd, load_sem.at[3]),
        pltpu.make_async_copy(back_hbm, back, load_sem.at[4]),
    ]
    for copy in loads + table_loads:
        copy.start()

    barrier = pltpu.get_barrier_semaphore()

    def other(d):
        return lax.rem(me + d, n)

    def greet(device):
        pl.semaphore_signal(barrier, inc=1, device_id=device, device_id_type=MESH)

    right, left = other(1), other(n - 1)

    @pl.when(end)
    def _():
        for d in range(1, n):
            greet({"phi": other(d)})

    @pl.when(jnp.logical_not(end))
    def _():
        greet({"phi": right})
        greet({"phi": left})

    @pl.when(t > 0)
    def _():
        greet({"theta": t - 1})

    @pl.when(t < nt - 1)
    def _():
        greet({"theta": t + 1})

    @pl.when(end)
    def _():
        pl.semaphore_wait(barrier, n)

    @pl.when(jnp.logical_not(end))
    def _():
        pl.semaphore_wait(barrier, 4)

    for copy in loads:
        copy.wait()

    def slot_place(owner, g):
        slot = owner * per + 2 * g
        return lax.div(slot, CAP), cap0 + lax.rem(slot, CAP)

    def remote(src, dst, send, recv, device):
        return pltpu.make_async_remote_copy(
            src_ref=src, dst_ref=dst, send_sem=send, recv_sem=recv,
            device_id=device, device_id_type=MESH,
        )

    def forward_copy(g, d):
        q = other(d)
        ch, r = slot_place(q, g)
        src = ext.at[ch, pl.ds(r, 2), main]
        dst = cyc.at[pl.ds(2 * g, 2), pl.ds(pl.multiple_of(me * cols, 8), cols)]
        if d == 0:
            return pltpu.make_async_copy(src, dst, fr.at[g, 0])
        return remote(src, dst, fs.at[g, d], fr.at[g, d], {"phi": q})

    def return_copy(g, d):
        q = other(d)
        src = fil.at[pl.ds(2 * g, 2), q]
        dst = caps.at[pl.ds(me * per + 2 * g, 2)]
        if d == 0:
            return pltpu.make_async_copy(src, dst, rr.at[g, 0])
        return remote(src, dst, rs.at[g, d], rr.at[g, d], {"phi": q})

    def ghost_copy(slot, channel, ghost_row, d, send, recv):
        q = other(d)
        src = fil.at[slot, other(d + n // 2)]
        dst = ext.at[channel, ghost_row]
        if d == 0:
            return pltpu.make_async_copy(src, dst, recv.at[0])
        return remote(src, dst, send.at[d], recv.at[d], {"phi": q})

    for c in range(CHANNELS):
        to_right[c] = ext[c, 0:rows, cols - 1]
        to_left[c] = ext[c, 0:rows, 0]
    to_left[CHANNELS] = ext[BPHI, 0:rows, 1]

    @pl.when(end)
    def _():
        for g in range(groups):
            for d in range(n):
                forward_copy(g, d).start()

    go_right = remote(to_right, at_left, hs.at[0], hr.at[0], {"phi": right})
    go_left = remote(to_left, at_right, hs.at[1], hr.at[1], {"phi": left})
    go_right.start()
    go_left.start()
    go_right.wait()
    go_left.wait()

    def unpack(lo, hi):
        for c in range(CHANNELS):
            ext[c, lo:hi, wide - 1] = at_left[c, lo:hi]
            ext[c, lo:hi, cols] = at_right[c, lo:hi]
        ext[BPHI, lo:hi, cols + 1] = at_right[CHANNELS, lo:hi]

    @pl.when(north)
    def _():
        unpack(CAP, rows)

    @pl.when(south)
    def _():
        unpack(0, rows - CAP)

    @pl.when(jnp.logical_not(end))
    def _():
        unpack(0, rows)

    every = pl.ds(0, CHANNELS)
    down = remote(ext.at[every, rows - 1], ext.at[every, rows + 2], ts.at[0], tr.at[0], {"theta": t + 1})
    up = remote(ext.at[every, 0], ext.at[every, rows], ts.at[1], tr.at[1], {"theta": t - 1})
    up2 = remote(ext.at[BTHETA, 1], ext.at[BTHETA, rows + 1], ts.at[2], tr.at[2], {"theta": t - 1})

    @pl.when(t < nt - 1)
    def _():
        down.start()

    @pl.when(t > 0)
    def _():
        up.start()
        up2.start()

    @pl.when(t > 0)
    def _():
        down.wait_recv()

    @pl.when(t < nt - 1)
    def _():
        up.wait_recv()
        up2.wait_recv()

    def sweep(lo, hi):
        def body(row, carry):
            stencil_row(ext, dout, bout, row, rows, cols)
            return carry

        lax.fori_loop(lo, hi, body, 0)

    early_lo = jnp.where(north, CAP + 1, 0)
    early_hi = jnp.where(south, rows - CAP - 2, rows)
    sweep(early_lo, early_hi)
    for copy in table_loads:
        copy.wait()

    @pl.when(end)
    def _():
        pole = jnp.where(north, 0, 1)
        mode = lax.rem(lax.broadcasted_iota(jnp.int32, (2 * KMAX, 128), 0), KMAX)
        weight = jnp.where(mode == 0, 1.0 / cycle, 2.0 / cycle)
        for g in range(groups):
            for d in range(n):
                copy = forward_copy(g, d)
                copy.wait() if d == 0 else copy.wait_recv()
            masks = []
            for s in (2 * g, 2 * g + 1):
                limit = lax.shift_right_logical(jnp.int32(KMAX), levels[pole, lax.rem(me * per + s, CAP)])
                masks.append(jnp.where(mode < limit, weight, 0.0))
            both = jnp.concatenate([cyc[2 * g], cyc[2 * g + 1]], axis=1)
            coeffs = product(fwd, both) * jnp.concatenate(masks, axis=1)
            values = product(back, coeffs)
            fil[2 * g] = values[:, :128].reshape(n, wide, 128)
            fil[2 * g + 1] = values[:, 128:].reshape(n, wide, 128)
            for d in range(n):
                return_copy(g, d).start()

    south_slot = per - 1
    second = BTHETA * CAP + CAP - 2
    second_owner, second_slot = second // per, second % per

    def north_ghost(owner, d):
        return ghost_copy(0, lax.div(owner * per, CAP), rows + 2, d, gs, gr)

    def south_ghost(owner, d):
        return ghost_copy(south_slot, lax.div(owner * per, CAP), rows, d, gs, gr)

    def second_ghost(d):
        return ghost_copy(second_slot, BTHETA, rows + 1, d, g2s, g2r)

    def has_first(owner):
        return lax.rem(owner * per, CAP) == 0

    def has_last(owner):
        return lax.rem(owner * per + per - 1, CAP) == CAP - 1

    @pl.when(north & has_first(me))
    def _():
        for d in range(n):
            north_ghost(me, d).start()

    @pl.when(south & has_last(me))
    def _():
        for d in range(n):
            south_ghost(me, d).start()

    @pl.when(south & (me == second_owner))
    def _():
        for d in range(n):
            second_ghost(d).start()

    @pl.when(end)
    def _():
        for g in range(groups):
            for d in range(1, n):
                forward_copy(g, d).wait_send()
            for d in range(n):
                copy = return_copy(g, d)
                copy.wait() if d == 0 else copy.wait_recv()

        def place(slot, carry):
            ext[lax.div(slot, CAP), cap0 + lax.rem(slot, CAP)] = caps[slot]
            return carry

        lax.fori_loop(0, CHANNELS * CAP, place, 0)

    for d in range(n):
        source = other(n - d)

        @pl.when(north & has_first(source))
        def _():
            copy = north_ghost(source, d)
            copy.wait() if d == 0 else copy.wait_recv()

        @pl.when(south & has_last(source))
        def _():
            copy = south_ghost(source, d)
            copy.wait() if d == 0 else copy.wait_recv()

        @pl.when(south & (source == second_owner))
        def _():
            copy = second_ghost(d)
            copy.wait() if d == 0 else copy.wait_recv()

    @pl.when(north)
    def _():
        for c in ODD:
            ext[c, rows + 2] = -ext[c, rows + 2]

    @pl.when(south)
    def _():
        for c in ODD:
            ext[c, rows] = -ext[c, rows]
        ext[BTHETA, rows + 1] = -ext[BTHETA, rows + 1]

    late_lo = jnp.where(south, rows - CAP - 2, 0)
    late_hi = jnp.where(north, CAP + 1, jnp.where(south, rows, 0))
    sweep(late_lo, late_hi)

    @pl.when(t < nt - 1)
    def _():
        down.wait_send()

    @pl.when(t > 0)
    def _():
        up.wait_send()
        up2.wait_send()

    @pl.when(end)
    def _():
        for g in range(groups):
            for d in range(1, n):
                return_copy(g, d).wait_send()

    @pl.when(north & has_first(me))
    def _():
        for d in range(1, n):
            north_ghost(me, d).wait_send()

    @pl.when(south & has_last(me))
    def _():
        for d in range(1, n):
            south_ghost(me, d).wait_send()

    @pl.when(south & (me == second_owner))
    def _():
        for d in range(1, n):
            second_ghost(d).wait_send()


def local(n, nt, density, velocity, bfield, levels):
    _, rows, cols, radial = density.shape
    per = CHANNELS * CAP // n
    groups = per // 2
    wide = cols + 8
    forward, back = tables(n, cols)
    any_space = pl.BlockSpec(memory_space=pl.ANY)
    vmem = pl.BlockSpec(memory_space=pltpu.VMEM)
    f32 = jnp.float32
    dma = pltpu.SemaphoreType.DMA
    return pl.pallas_call(
        functools.partial(kernel, n, nt, rows, cols),
        out_shape=(
            jax.ShapeDtypeStruct(density.shape, f32),
            jax.ShapeDtypeStruct(bfield.shape, f32),
        ),
        in_specs=[any_space] * 3 + [pl.BlockSpec(memory_space=pltpu.SMEM)] + [any_space] * 2,
        out_specs=(vmem, vmem),
        scratch_shapes=[
            pltpu.VMEM((CHANNELS, rows + 3, wide, radial), f32),
            pltpu.VMEM((per, n * cols, radial), f32),
            pltpu.VMEM((per, n, wide, radial), f32),
            pltpu.VMEM((CHANNELS * CAP, wide, radial), f32),
            pltpu.VMEM(forward.shape, jnp.bfloat16),
            pltpu.VMEM(back.shape, jnp.bfloat16),
            pltpu.VMEM((CHANNELS, rows, radial), f32),
            pltpu.VMEM((CHANNELS + 1, rows, radial), f32),
            pltpu.VMEM((CHANNELS, rows, radial), f32),
            pltpu.VMEM((CHANNELS + 1, rows, radial), f32),
            dma((5,)),
            dma((groups, n)),
            dma((groups, n)),
            dma((groups, n)),
            dma((groups, n)),
            dma((n,)),
            dma((n,)),
            dma((n,)),
            dma((n,)),
            dma((2,)),
            dma((2,)),
            dma((3,)),
            dma((3,)),
        ],
        compiler_params=pltpu.CompilerParams(
            collective_id=0, has_side_effects=True, vmem_limit_bytes=40 * 1024 * 1024
        ),
        name="substep",
    )(density, velocity, bfield, levels, jnp.asarray(forward), jnp.asarray(back))


def solution(mesh):
    spec = P(None, "theta", "phi", None)
    return jax.shard_map(
        functools.partial(local, mesh.shape["phi"], mesh.shape["theta"]),
        mesh=mesh,
        in_specs=(spec, spec, spec, P()),
        out_specs=(spec, spec),
        check_vma=False,
    )
```

```python
import functools
import math

import jax
import jax.numpy as jnp
import numpy as np
import ml_dtypes
from jax import lax
from jax.experimental import pallas as pl
from jax.experimental.pallas import tpu as pltpu
from jax.sharding import PartitionSpec as P

CAP = 4
KMAX = 128
TIME_STEP = 0.2
CHANNELS = 8
ODD = (3, 4, 6, 7)
BTHETA = 6
BPHI = 7
MESH = pl.DeviceIdType.MESH


def split_table(table):
    high = table.astype(ml_dtypes.bfloat16)
    low = (table - high.astype(np.float64)).astype(ml_dtypes.bfloat16)
    return np.stack([high, low])


def tables(count, cols):
    cycle = count * cols
    orders = np.arange(KMAX)
    points = np.arange(cycle)
    angle = (orders[:, None] * points[None, :] % cycle) * (2.0 * math.pi / cycle)
    forward = np.concatenate([np.cos(angle), np.sin(angle)], axis=0)
    offset = np.concatenate([np.arange(cols + 7), [-1]])
    place = ((np.arange(count)[:, None] * cols + offset[None, :]) % cycle).reshape(-1)
    back = forward.T[place]
    return split_table(forward), split_table(back)


def flux(ql, qr, vl, vr):
    return 0.5 * (ql * vl + qr * vr) - 0.5 * jnp.maximum(jnp.abs(vl), jnp.abs(vr)) * (qr - ql)


def stencil_row(ext, dout, bout, row, rows, cols):
    wide = cols + 8
    lower = jnp.where(row == 0, rows + 2, row - 1)
    upper = row + 1
    upper2 = row + 2
    lane = lax.broadcasted_iota(jnp.int32, (wide, 128), 1)
    first = lane == 0
    last = lane == 127

    def from_left(x):
        return pltpu.roll(x, 1, 0)

    def from_right(x):
        return pltpu.roll(x, wide - 1, 0)

    def from_below(x):
        return pltpu.roll(x, 1, 1)

    def from_above(x):
        return pltpu.roll(x, 127, 1)

    vr, vt, vp = ext[2, row], ext[3, row], ext[4, row]
    vt_lo, vt_up = ext[3, lower], ext[3, upper]
    vp_l = from_left(vp)
    vr_b = jnp.where(first, vr, from_below(vr))
    for c in range(2):
        q = ext[c, row]
        tend = flux(q, ext[c, upper], vt, vt_up) - flux(ext[c, lower], q, vt_lo, vt)
        fp = flux(from_left(q), q, vp_l, vp)
        tend = tend + from_right(fp) - fp
        fr = flux(jnp.where(first, q, from_below(q)), q, vr_b, vr)
        tend = tend + jnp.where(last, q * vr, from_above(fr)) - fr
        new = q - TIME_STEP * tend
        dout[c, row] = new[:cols]

    def emfs(j, bt_next):
        ur, ut, up = ext[2, j], ext[3, j], ext[4, j]
        br, bt, bp = ext[5, j], ext[6, j], ext[7, j]
        br_c = 0.5 * (br + jnp.where(last, br, from_above(br)))
        bt_c = 0.5 * (bt + bt_next)
        bp_c = 0.5 * (bp + from_right(bp))
        e_r = -(ut * bp_c - up * bt_c)
        e_p = -(ur * bt_c - ut * br_c)
        e_p0 = -(ur * bt_c - ut * br)
        pair_p = e_p + jnp.where(first, e_p0, from_below(e_p))
        pair_r = e_r + from_left(e_r)
        return e_p, pair_p, pair_r, br_c, bp_c

    bt = ext[6, row]
    bt_up = ext[6, upper]
    ep_lo, pp_lo, pr_lo, _, _ = emfs(lower, bt)
    ep, pp, pr, br_c, bp_c = emfs(row, bt_up)
    ep_up, pp_up, pr_up, _, _ = emfs(upper, ext[6, upper2])
    br = ext[5, row]
    e_t = -(vp * br_c - vr * bp_c)
    e_t0 = -(vp * br - vr * bp_c)
    et_pair = e_t + from_left(e_t)
    et_pair0 = e_t0 + from_left(e_t0)
    edge_t = et_pair + jnp.where(first, et_pair0, from_below(et_pair))
    edge_t_above = jnp.where(last, 2.0 * et_pair, from_above(edge_t))
    edge_p = pp_lo + pp
    edge_p_above = jnp.where(last, 2.0 * (ep_lo + ep), from_above(edge_p))
    edge_r = pr_lo + pr
    scale = TIME_STEP * 0.25
    new_r = br - scale * ((pp_up - pp_lo) - (from_right(edge_t) - edge_t))
    new_t = bt - scale * ((from_right(edge_r) - edge_r) - (edge_p_above - edge_p))
    new_p = ext[7, row] - scale * ((edge_t_above - edge_t) - (pr_up - pr_lo))
    bout[0, row] = new_r[:cols]
    bout[1, row] = new_t[:cols]
    bout[2, row] = new_p[:cols]


def split(x):
    high = x.astype(jnp.bfloat16)
    return high, (x - high.astype(jnp.float32)).astype(jnp.bfloat16)


def product(table, x):
    high, low = split(x)
    dot = functools.partial(jnp.dot, preferred_element_type=jnp.float32)
    return dot(table[0], high) + (dot(table[0], low) + dot(table[1], high))


def kernel(
    n, nt, rows, cols,
    density, velocity, bfield, levels, fwd_hbm, back_hbm,
    dout, bout,
    ext, cyc, fil, caps, fwd, back, to_right, to_left, at_left, at_right,
    load_sem, fs, fr, rs, rr, gs, gr, g2s, g2r, hs, hr, ts, tr,
):
    per = CHANNELS * CAP // n
    groups = per // 2
    wide = cols + 8
    cycle = n * cols
    t = lax.axis_index("theta")
    me = lax.axis_index("phi")
    north = t == 0
    south = t == nt - 1
    end = north | south
    cap0 = jnp.where(north, 0, rows - CAP)
    main = pl.ds(0, cols)

    loads = [
        pltpu.make_async_copy(density, ext.at[pl.ds(0, 2), pl.ds(0, rows), main], load_sem.at[0]),
        pltpu.make_async_copy(velocity, ext.at[pl.ds(2, 3), pl.ds(0, rows), main], load_sem.at[1]),
        pltpu.make_async_copy(bfield, ext.at[pl.ds(5, 3), pl.ds(0, rows), main], load_sem.at[2]),
    ]
    table_loads = [
        pltpu.make_async_copy(fwd_hbm, fwd, load_sem.at[3]),
        pltpu.make_async_copy(back_hbm, back, load_sem.at[4]),
    ]
    for copy in loads + table_loads:
        copy.start()

    barrier = pltpu.get_barrier_semaphore()

    def other(d):
        return lax.rem(me + d, n)

    def greet(device):
        pl.semaphore_signal(barrier, inc=1, device_id=device, device_id_type=MESH)

    right, left = other(1), other(n - 1)

    @pl.when(end)
    def _():
        for d in range(1, n):
            greet({"phi": other(d)})

    @pl.when(jnp.logical_not(end))
    def _():
        greet({"phi": right})
        greet({"phi": left})

    @pl.when(t > 0)
    def _():
        greet({"theta": t - 1})

    @pl.when(t < nt - 1)
    def _():
        greet({"theta": t + 1})

    @pl.when(end)
    def _():
        pl.semaphore_wait(barrier, n)

    @pl.when(jnp.logical_not(end))
    def _():
        pl.semaphore_wait(barrier, 4)

    for copy in loads:
        copy.wait()

    def cap_row(slot):
        row = lax.rem(slot, CAP)
        return jnp.where(north, CAP - 2 - row, row)

    def slot_place(owner, g):
        slot = owner * per + 2 * g
        return lax.div(slot, CAP), cap0 + cap_row(slot)

    def remote(src, dst, send, recv, device):
        return pltpu.make_async_remote_copy(
            src_ref=src, dst_ref=dst, send_sem=send, recv_sem=recv,
            device_id=device, device_id_type=MESH,
        )

    def forward_copy(g, d):
        q = other(d)
        ch, r = slot_place(q, g)
        src = ext.at[ch, pl.ds(r, 2), main]
        dst = cyc.at[pl.ds(2 * g, 2), pl.ds(pl.multiple_of(me * cols, 8), cols)]
        if d == 0:
            return pltpu.make_async_copy(src, dst, fr.at[g, 0])
        return remote(src, dst, fs.at[g, d], fr.at[g, d], {"phi": q})

    def return_copy(g, d):
        q = other(d)
        src = fil.at[pl.ds(2 * g, 2), q]
        dst = caps.at[pl.ds(me * per + 2 * g, 2)]
        if d == 0:
            return pltpu.make_async_copy(src, dst, rr.at[g, 0])
        return remote(src, dst, rs.at[g, d], rr.at[g, d], {"phi": q})

    def ghost_copy(slot, channel, ghost_row, d, send, recv):
        q = other(d)
        src = fil.at[slot, other(d + n // 2)]
        dst = ext.at[channel, ghost_row]
        if d == 0:
            return pltpu.make_async_copy(src, dst, recv.at[0])
        return remote(src, dst, send.at[d], recv.at[d], {"phi": q})

    far_first = sorted(range(n), key=lambda d: -min(d, n - d))

    for c in range(CHANNELS):
        to_right[c] = ext[c, 0:rows, cols - 1]
        to_left[c] = ext[c, 0:rows, 0]
    to_left[CHANNELS] = ext[BPHI, 0:rows, 1]

    go_right = remote(to_right, at_left, hs.at[0], hr.at[0], {"phi": right})
    go_left = remote(to_left, at_right, hs.at[1], hr.at[1], {"phi": left})
    go_right.start()
    go_left.start()

    @pl.when(end)
    def _():
        for g in range(groups):
            for d in far_first:
                forward_copy(g, d).start()

    go_right.wait()
    go_left.wait()

    def unpack(lo, hi):
        for c in range(CHANNELS):
            ext[c, lo:hi, wide - 1] = at_left[c, lo:hi]
            ext[c, lo:hi, cols] = at_right[c, lo:hi]
        ext[BPHI, lo:hi, cols + 1] = at_right[CHANNELS, lo:hi]

    @pl.when(north)
    def _():
        unpack(CAP, rows)

    @pl.when(south)
    def _():
        unpack(0, rows - CAP)

    @pl.when(jnp.logical_not(end))
    def _():
        unpack(0, rows)

    every = pl.ds(0, CHANNELS)
    down = remote(ext.at[every, rows - 1], ext.at[every, rows + 2], ts.at[0], tr.at[0], {"theta": t + 1})
    up = remote(ext.at[every, 0], ext.at[every, rows], ts.at[1], tr.at[1], {"theta": t - 1})
    up2 = remote(ext.at[BTHETA, 1], ext.at[BTHETA, rows + 1], ts.at[2], tr.at[2], {"theta": t - 1})

    @pl.when(t < nt - 1)
    def _():
        down.start()

    @pl.when(t > 0)
    def _():
        up.start()
        up2.start()

    @pl.when(t > 0)
    def _():
        down.wait_recv()

    @pl.when(t < nt - 1)
    def _():
        up.wait_recv()
        up2.wait_recv()

    def sweep(lo, hi):
        def body(row, carry):
            stencil_row(ext, dout, bout, row, rows, cols)
            return carry

        lax.fori_loop(lo, hi, body, 0)

    early_lo = jnp.where(north, CAP + 1, 0)
    early_hi = jnp.where(south, rows - CAP - 2, rows)
    sweep(early_lo, early_hi)
    for copy in table_loads:
        copy.wait()

    @pl.when(end)
    def _():
        pole = jnp.where(north, 0, 1)
        mode = lax.rem(lax.broadcasted_iota(jnp.int32, (2 * KMAX, 128), 0), KMAX)
        weight = jnp.where(mode == 0, 1.0 / cycle, 2.0 / cycle)
        for g in range(groups):
            for d in range(n):
                copy = forward_copy(g, d)
                copy.wait() if d == 0 else copy.wait_recv()
            masks = []
            for s in (2 * g, 2 * g + 1):
                limit = lax.shift_right_logical(jnp.int32(KMAX), levels[pole, cap_row(me * per + 2 * g) + s - 2 * g])
                masks.append(jnp.where(mode < limit, weight, 0.0))
            both = jnp.concatenate([cyc[2 * g], cyc[2 * g + 1]], axis=1)
            coeffs = product(fwd, both) * jnp.concatenate(masks, axis=1)
            values = product(back, coeffs)
            fil[2 * g] = values[:, :128].reshape(n, wide, 128)
            fil[2 * g + 1] = values[:, 128:].reshape(n, wide, 128)
            for d in far_first:
                return_copy(g, d).start()

    north_slot = per - 2
    south_slot = per - 1
    second = BTHETA * CAP + CAP - 2
    second_owner, second_slot = second // per, second % per

    def north_ghost(owner, d):
        return ghost_copy(north_slot, lax.div(owner * per, CAP), rows + 2, d, gs, gr)

    def south_ghost(owner, d):
        return ghost_copy(south_slot, lax.div(owner * per, CAP), rows, d, gs, gr)

    def second_ghost(d):
        return ghost_copy(second_slot, BTHETA, rows + 1, d, g2s, g2r)

    def has_edge(owner):
        return lax.rem(owner * per + per, CAP) == 0

    @pl.when(north & has_edge(me))
    def _():
        for d in range(n):
            north_ghost(me, d).start()

    @pl.when(south & has_edge(me))
    def _():
        for d in range(n):
            south_ghost(me, d).start()

    @pl.when(south & (me == second_owner))
    def _():
        for d in range(n):
            second_ghost(d).start()

    @pl.when(end)
    def _():
        for g in range(groups):
            for d in range(1, n):
                forward_copy(g, d).wait_send()

    def take(g):
        for d in range(n):
            copy = return_copy(g, d)
            copy.wait() if d == 0 else copy.wait_recv()

        def place(owner, carry):
            ch, r = slot_place(owner, g)
            ext[ch, r] = caps[owner * per + 2 * g]
            ext[ch, r + 1] = caps[owner * per + 2 * g + 1]
            return carry

        lax.fori_loop(0, n, place, 0)

    for g in range(groups):

        @pl.when(end)
        def _():
            take(g)
            if groups == 2 and g == 0:
                sweep(jnp.where(north, CAP - 1, rows - CAP - 2), jnp.where(north, CAP + 1, rows - CAP))

    for d in range(n):
        source = other(n - d)

        @pl.when(north & has_edge(source))
        def _():
            copy = north_ghost(source, d)
            copy.wait() if d == 0 else copy.wait_recv()

        @pl.when(south & has_edge(source))
        def _():
            copy = south_ghost(source, d)
            copy.wait() if d == 0 else copy.wait_recv()

        @pl.when(south & (source == second_owner))
        def _():
            copy = second_ghost(d)
            copy.wait() if d == 0 else copy.wait_recv()

    @pl.when(north)
    def _():
        for c in ODD:
            ext[c, rows + 2] = -ext[c, rows + 2]

    @pl.when(south)
    def _():
        for c in ODD:
            ext[c, rows] = -ext[c, rows]
        ext[BTHETA, rows + 1] = -ext[BTHETA, rows + 1]

    late_lo = jnp.where(south, rows - CAP - 2 if groups != 2 else rows - CAP, 0)
    late_hi = jnp.where(north, CAP + 1 if groups != 2 else CAP - 1, jnp.where(south, rows, 0))
    sweep(late_lo, late_hi)

    @pl.when(t < nt - 1)
    def _():
        down.wait_send()

    @pl.when(t > 0)
    def _():
        up.wait_send()
        up2.wait_send()

    @pl.when(end)
    def _():
        for g in range(groups):
            for d in range(1, n):
                return_copy(g, d).wait_send()

    @pl.when(north & has_edge(me))
    def _():
        for d in range(1, n):
            north_ghost(me, d).wait_send()

    @pl.when(south & has_edge(me))
    def _():
        for d in range(1, n):
            south_ghost(me, d).wait_send()

    @pl.when(south & (me == second_owner))
    def _():
        for d in range(1, n):
            second_ghost(d).wait_send()


def local(n, nt, density, velocity, bfield, levels):
    _, rows, cols, radial = density.shape
    per = CHANNELS * CAP // n
    groups = per // 2
    wide = cols + 8
    forward, back = tables(n, cols)
    any_space = pl.BlockSpec(memory_space=pl.ANY)
    vmem = pl.BlockSpec(memory_space=pltpu.VMEM)
    f32 = jnp.float32
    dma = pltpu.SemaphoreType.DMA
    return pl.pallas_call(
        functools.partial(kernel, n, nt, rows, cols),
        out_shape=(
            jax.ShapeDtypeStruct(density.shape, f32),
            jax.ShapeDtypeStruct(bfield.shape, f32),
        ),
        in_specs=[any_space] * 3 + [pl.BlockSpec(memory_space=pltpu.SMEM)] + [any_space] * 2,
        out_specs=(vmem, vmem),
        scratch_shapes=[
            pltpu.VMEM((CHANNELS, rows + 3, wide, radial), f32),
            pltpu.VMEM((per, n * cols, radial), f32),
            pltpu.VMEM((per, n, wide, radial), f32),
            pltpu.VMEM((CHANNELS * CAP, wide, radial), f32),
            pltpu.VMEM(forward.shape, jnp.bfloat16),
            pltpu.VMEM(back.shape, jnp.bfloat16),
            pltpu.VMEM((CHANNELS, rows, radial), f32),
            pltpu.VMEM((CHANNELS + 1, rows, radial), f32),
            pltpu.VMEM((CHANNELS, rows, radial), f32),
            pltpu.VMEM((CHANNELS + 1, rows, radial), f32),
            dma((5,)),
            dma((groups, n)),
            dma((groups, n)),
            dma((groups, n)),
            dma((groups, n)),
            dma((n,)),
            dma((n,)),
            dma((n,)),
            dma((n,)),
            dma((2,)),
            dma((2,)),
            dma((3,)),
            dma((3,)),
        ],
        compiler_params=pltpu.CompilerParams(
            collective_id=0, has_side_effects=True, vmem_limit_bytes=60 * 1024 * 1024
        ),
        name="substep",
    )(density, velocity, bfield, levels, jnp.asarray(forward), jnp.asarray(back))


def solution(mesh):
    spec = P(None, "theta", "phi", None)
    return jax.shard_map(
        functools.partial(local, mesh.shape["phi"], mesh.shape["theta"]),
        mesh=mesh,
        in_specs=(spec, spec, spec, P()),
        out_specs=(spec, spec),
        check_vma=False,
    )
```

```python
import functools
import math

import jax
import jax.numpy as jnp
import numpy as np
import ml_dtypes
from jax import lax
from jax.experimental import pallas as pl
from jax.experimental.pallas import tpu as pltpu
from jax.sharding import PartitionSpec as P

CAP = 4
KMAX = 128
TIME_STEP = 0.2
CHANNELS = 8
HUBS = 2
ODD = (3, 4, 6, 7)
BTHETA = 6
BPHI = 7
MESH = pl.DeviceIdType.MESH


def split_table(table):
    high = table.astype(ml_dtypes.bfloat16)
    low = (table - high.astype(np.float64)).astype(ml_dtypes.bfloat16)
    return np.stack([high, low])


def tables(count, cols):
    cycle = count * cols
    orders = np.arange(KMAX)
    points = np.arange(cycle)
    angle = (orders[:, None] * points[None, :] % cycle) * (2.0 * math.pi / cycle)
    forward = np.concatenate([np.cos(angle), np.sin(angle)], axis=0)
    offset = np.concatenate([np.arange(cols + 7), [-1]])
    place = ((np.arange(count)[:, None] * cols + offset[None, :]) % cycle).reshape(-1)
    back = forward.T[place]
    return split_table(forward), split_table(back)


def flux(ql, qr, vl, vr):
    return 0.5 * (ql * vl + qr * vr) - 0.5 * jnp.maximum(jnp.abs(vl), jnp.abs(vr)) * (qr - ql)


def stencil_row(ext, dout, bout, row, rows, cols):
    wide = cols + 8
    lower = jnp.where(row == 0, rows + 2, row - 1)
    upper = row + 1
    upper2 = row + 2
    lane = lax.broadcasted_iota(jnp.int32, (wide, 128), 1)
    first = lane == 0
    last = lane == 127

    def from_left(x):
        return pltpu.roll(x, 1, 0)

    def from_right(x):
        return pltpu.roll(x, wide - 1, 0)

    def from_below(x):
        return pltpu.roll(x, 1, 1)

    def from_above(x):
        return pltpu.roll(x, 127, 1)

    vr, vt, vp = ext[2, row], ext[3, row], ext[4, row]
    vt_lo, vt_up = ext[3, lower], ext[3, upper]
    vp_l = from_left(vp)
    vr_b = jnp.where(first, vr, from_below(vr))
    for c in range(2):
        q = ext[c, row]
        tend = flux(q, ext[c, upper], vt, vt_up) - flux(ext[c, lower], q, vt_lo, vt)
        fp = flux(from_left(q), q, vp_l, vp)
        tend = tend + from_right(fp) - fp
        fr = flux(jnp.where(first, q, from_below(q)), q, vr_b, vr)
        tend = tend + jnp.where(last, q * vr, from_above(fr)) - fr
        new = q - TIME_STEP * tend
        dout[c, row] = new[:cols]

    def emfs(j, bt_next):
        ur, ut, up = ext[2, j], ext[3, j], ext[4, j]
        br, bt, bp = ext[5, j], ext[6, j], ext[7, j]
        br_c = 0.5 * (br + jnp.where(last, br, from_above(br)))
        bt_c = 0.5 * (bt + bt_next)
        bp_c = 0.5 * (bp + from_right(bp))
        e_r = -(ut * bp_c - up * bt_c)
        e_p = -(ur * bt_c - ut * br_c)
        e_p0 = -(ur * bt_c - ut * br)
        pair_p = e_p + jnp.where(first, e_p0, from_below(e_p))
        pair_r = e_r + from_left(e_r)
        return e_p, pair_p, pair_r, br_c, bp_c

    bt = ext[6, row]
    bt_up = ext[6, upper]
    ep_lo, pp_lo, pr_lo, _, _ = emfs(lower, bt)
    ep, pp, pr, br_c, bp_c = emfs(row, bt_up)
    ep_up, pp_up, pr_up, _, _ = emfs(upper, ext[6, upper2])
    br = ext[5, row]
    e_t = -(vp * br_c - vr * bp_c)
    e_t0 = -(vp * br - vr * bp_c)
    et_pair = e_t + from_left(e_t)
    et_pair0 = e_t0 + from_left(e_t0)
    edge_t = et_pair + jnp.where(first, et_pair0, from_below(et_pair))
    edge_t_above = jnp.where(last, 2.0 * et_pair, from_above(edge_t))
    edge_p = pp_lo + pp
    edge_p_above = jnp.where(last, 2.0 * (ep_lo + ep), from_above(edge_p))
    edge_r = pr_lo + pr
    scale = TIME_STEP * 0.25
    new_r = br - scale * ((pp_up - pp_lo) - (from_right(edge_t) - edge_t))
    new_t = bt - scale * ((from_right(edge_r) - edge_r) - (edge_p_above - edge_p))
    new_p = ext[7, row] - scale * ((edge_t_above - edge_t) - (pr_up - pr_lo))
    bout[0, row] = new_r[:cols]
    bout[1, row] = new_t[:cols]
    bout[2, row] = new_p[:cols]


def split(x):
    high = x.astype(jnp.bfloat16)
    return high, (x - high.astype(jnp.float32)).astype(jnp.bfloat16)


def product(table, x):
    high, low = split(x)
    dot = functools.partial(jnp.dot, preferred_element_type=jnp.float32)
    return dot(table[0], high) + (dot(table[0], low) + dot(table[1], high))


def kernel(
    n, nt, rows, cols,
    density, velocity, bfield, levels, fwd_hbm, back_hbm,
    dout, bout,
    ext, cyc, part, other_part, fil, gfil, caps, fwd, back, to_right, to_left, at_left, at_right,
    load_sem, fs, fr, ms, mr, rs, rr, gs, gr, g2s, g2r, hs, hr, ts, tr,
):
    half_n = n // 2
    groups = CHANNELS // HUBS * 2
    pole_groups = groups // 2
    wide = cols + 8
    cycle = n * cols
    t = lax.axis_index("theta")
    me = lax.axis_index("phi")
    north = t == 0
    south = t == nt - 1
    end = north | south
    cap0 = jnp.where(north, 0, rows - CAP)
    main = pl.ds(0, cols)
    half = lax.div(me, half_n)
    place = lax.rem(me, half_n)

    def hub_place(j):
        return jnp.where(half == 0, half_n - HUBS + j, j)

    hub_index = place - hub_place(0)
    hub = end & (hub_index >= 0) & (hub_index < HUBS)

    loads = [
        pltpu.make_async_copy(density, ext.at[pl.ds(0, 2), pl.ds(0, rows), main], load_sem.at[0]),
        pltpu.make_async_copy(velocity, ext.at[pl.ds(2, 3), pl.ds(0, rows), main], load_sem.at[1]),
        pltpu.make_async_copy(bfield, ext.at[pl.ds(5, 3), pl.ds(0, rows), main], load_sem.at[2]),
    ]
    width = half_n * wide
    near = pl.ds(pl.multiple_of(half * width, 16), width)
    far = pl.ds(pl.multiple_of((1 - half) * width, 16), width)
    mine = pl.ds(pl.multiple_of(half * half_n * cols, 128), half_n * cols)
    both = pl.ds(0, 2)
    modes = pl.ds(0, 2 * KMAX)
    table_loads = [
        pltpu.make_async_copy(fwd_hbm.at[both, modes, mine], fwd, load_sem.at[3]),
        pltpu.make_async_copy(back_hbm.at[both, near], back.at[0], load_sem.at[4]),
        pltpu.make_async_copy(back_hbm.at[both, far], back.at[1], load_sem.at[5]),
    ]
    for copy in loads + table_loads:
        copy.start()

    barrier = pltpu.get_barrier_semaphore()

    def other(d):
        return lax.rem(me + d, n)

    def greet(device):
        pl.semaphore_signal(barrier, inc=1, device_id=device, device_id_type=MESH)

    right, left = other(1), other(n - 1)

    @pl.when(end)
    def _():
        for d in range(1, n):
            greet({"phi": other(d)})

    @pl.when(jnp.logical_not(end))
    def _():
        greet({"phi": right})
        greet({"phi": left})

    @pl.when(t > 0)
    def _():
        greet({"theta": t - 1})

    @pl.when(t < nt - 1)
    def _():
        greet({"theta": t + 1})

    @pl.when(end)
    def _():
        pl.semaphore_wait(barrier, n)

    @pl.when(jnp.logical_not(end))
    def _():
        pl.semaphore_wait(barrier, 4)

    for copy in loads:
        copy.wait()

    def remote(src, dst, send, recv, device):
        return pltpu.make_async_remote_copy(
            src_ref=src, dst_ref=dst, send_sem=send, recv_sem=recv,
            device_id=device, device_id_type=MESH,
        )

    def await_bytes(ref, sem):
        pltpu.make_async_copy(ref, ref, sem).wait()

    def repeat(count, body):
        def step(i, carry):
            body(i)
            return carry

        lax.fori_loop(0, count, step, 0)

    def cap_pair(g):
        later = lax.div(g, pole_groups)
        return jnp.where(north, CAP - 2 - 2 * later, 2 * later)

    def channel(j, g):
        return j * pole_groups + lax.rem(g, pole_groups)

    def cap_slots(j, g):
        return pl.ds(channel(j, g) * CAP + 2 * lax.div(g, pole_groups), 2)

    def forward_copy(j, g):
        src = ext.at[channel(j, g), pl.ds(cap0 + cap_pair(g), 2), main]
        dst = cyc.at[g, both, pl.ds(pl.multiple_of(place * cols, 8), cols)]
        device = half * half_n + hub_place(j)
        return (
            pltpu.make_async_copy(src, dst, fr.at[g, place]),
            remote(src, dst, fs.at[j, g], fr.at[g, place], {"phi": device}),
        )

    def middle_copy(g):
        partner = jnp.where(half == 0, half_n, half_n - HUBS) + hub_index
        return remote(part.at[g], other_part.at[g], ms.at[g], mr.at[g], {"phi": partner})

    def target(d):
        spot = lax.rem(place + d, half_n)
        return spot, half * half_n + spot

    def return_copy(g, d):
        spot, device = target(d)
        src = fil.at[g, both, spot]
        dst = caps.at[cap_slots(hub_index, g)]
        sem = rr.at[hub_index, g]
        if d == 0:
            return pltpu.make_async_copy(src, dst, sem)
        return remote(src, dst, rs.at[g, d], sem, {"phi": device})

    ghost_row = jnp.where(north, rows + 2, rows)

    def ghost_copy(g, d):
        spot, device = target(d)
        src = gfil.at[g, jnp.where(north, 0, 1), spot]
        dst = ext.at[channel(hub_index, g), ghost_row]
        sem = gr.at[hub_index, g]
        if d == 0:
            return pltpu.make_async_copy(src, dst, sem)
        return remote(src, dst, gs.at[g, d], sem, {"phi": device})

    second_hub, second_group = BTHETA // pole_groups, BTHETA % pole_groups

    def second_copy(d):
        spot, device = target(d)
        src = gfil.at[second_group, 0, spot]
        dst = ext.at[BTHETA, rows + 1]
        if d == 0:
            return pltpu.make_async_copy(src, dst, g2r.at[0])
        return remote(src, dst, g2s.at[d], g2r.at[0], {"phi": device})

    for c in range(CHANNELS):
        to_right[c] = ext[c, 0:rows, cols - 1]
        to_left[c] = ext[c, 0:rows, 0]
    to_left[CHANNELS] = ext[BPHI, 0:rows, 1]

    go_right = remote(to_right, at_left, hs.at[0], hr.at[0], {"phi": right})
    go_left = remote(to_left, at_right, hs.at[1], hr.at[1], {"phi": left})
    go_right.start()
    go_left.start()

    @pl.when(end)
    def _():
        def send(g):
            for j in range(HUBS):
                here, away = forward_copy(j, g)

                @pl.when(hub_place(j) == place)
                def _():
                    here.start()

                @pl.when(hub_place(j) != place)
                def _():
                    away.start()

        repeat(groups, send)

    go_right.wait()
    go_left.wait()

    def unpack(lo, hi):
        for c in range(CHANNELS):
            ext[c, lo:hi, wide - 1] = at_left[c, lo:hi]
            ext[c, lo:hi, cols] = at_right[c, lo:hi]
        ext[BPHI, lo:hi, cols + 1] = at_right[CHANNELS, lo:hi]

    @pl.when(north)
    def _():
        unpack(CAP, rows)

    @pl.when(south)
    def _():
        unpack(0, rows - CAP)

    @pl.when(jnp.logical_not(end))
    def _():
        unpack(0, rows)

    every = pl.ds(0, CHANNELS)
    down = remote(ext.at[every, rows - 1], ext.at[every, rows + 2], ts.at[0], tr.at[0], {"theta": t + 1})
    up = remote(ext.at[every, 0], ext.at[every, rows], ts.at[1], tr.at[1], {"theta": t - 1})
    up2 = remote(ext.at[BTHETA, 1], ext.at[BTHETA, rows + 1], ts.at[2], tr.at[2], {"theta": t - 1})

    @pl.when(t < nt - 1)
    def _():
        down.start()

    @pl.when(t > 0)
    def _():
        up.start()
        up2.start()

    for copy in table_loads:
        copy.wait()

    @pl.when(hub)
    def _():
        pole = jnp.where(north, 0, 1)
        mode = lax.rem(lax.broadcasted_iota(jnp.int32, (2 * KMAX, 128), 0), KMAX)
        weight = jnp.where(mode == 0, 1.0 / cycle, 2.0 / cycle)

        def analyse(g):
            for i in range(half_n):
                await_bytes(cyc.at[g, both, pl.ds(i * cols, cols)], fr.at[g, i])
            part[g] = product(fwd, jnp.concatenate([cyc[g, 0], cyc[g, 1]], axis=1))
            middle_copy(g).start()

        def evaluate(g):
            await_bytes(other_part.at[g], mr.at[g])
            masks = []
            for s in range(2):
                limit = lax.shift_right_logical(jnp.int32(KMAX), levels[pole, cap_pair(g) + s])
                masks.append(jnp.where(mode < limit, weight, 0.0))
            coeffs = (part[g] + other_part[g]) * jnp.concatenate(masks, axis=1)
            values = product(back[0], coeffs)
            fil[g, 0] = values[:, :128].reshape(half_n, wide, 128)
            fil[g, 1] = values[:, 128:].reshape(half_n, wide, 128)
            for d in reversed(range(half_n)):
                return_copy(g, d).start()

            @pl.when(g >= pole_groups)
            def _():
                k = g - pole_groups
                ghosts = product(back[1], coeffs)
                gfil[k, 0] = ghosts[:, :128].reshape(half_n, wide, 128)
                gfil[k, 1] = ghosts[:, 128:].reshape(half_n, wide, 128)
                for d in reversed(range(half_n)):
                    ghost_copy(k, d).start()

        def step(g):
            @pl.when(g < groups)
            def _():
                analyse(g)

            @pl.when(g >= 1)
            def _():
                evaluate(g - 1)

        repeat(groups + 1, step)

    @pl.when(south & hub & (hub_index == second_hub))
    def _():
        for d in range(half_n):
            second_copy(d).start()

    @pl.when(t > 0)
    def _():
        down.wait_recv()

    @pl.when(t < nt - 1)
    def _():
        up.wait_recv()
        up2.wait_recv()

    def sweep(lo, hi):
        def body(row, carry):
            stencil_row(ext, dout, bout, row, rows, cols)
            return carry

        lax.fori_loop(lo, hi, body, 0)

    early_lo = jnp.where(north, CAP + 1, 0)
    early_hi = jnp.where(south, rows - CAP - 2, rows)
    sweep(early_lo, early_hi)

    @pl.when(end)
    def _():
        def sent(g):
            for j in range(HUBS):
                @pl.when(hub_place(j) != place)
                def _():
                    forward_copy(j, g)[1].wait_send()

        repeat(groups, sent)

        def take(first):
            def one(k):
                g = first + k
                for j in range(HUBS):
                    slots = cap_slots(j, g)
                    await_bytes(caps.at[slots], rr.at[j, g])
                    c = channel(j, g)
                    slot = c * CAP + 2 * lax.div(g, pole_groups)
                    r = cap0 + cap_pair(g)
                    ext[c, r] = caps[slot]
                    ext[c, r + 1] = caps[slot + 1]

            repeat(pole_groups, one)

        take(0)
        sweep(jnp.where(north, CAP - 1, rows - CAP - 2), jnp.where(north, CAP + 1, rows - CAP))
        take(pole_groups)

        def ghost(k):
            for j in range(HUBS):
                await_bytes(ext.at[channel(j, k), ghost_row], gr.at[j, k])

        repeat(pole_groups, ghost)
        for c in ODD:
            ext[c, ghost_row] = -ext[c, ghost_row]

        @pl.when(south)
        def _():
            await_bytes(ext.at[BTHETA, rows + 1], g2r.at[0])
            ext[BTHETA, rows + 1] = -ext[BTHETA, rows + 1]

        sweep(jnp.where(north, 0, rows - CAP), jnp.where(north, CAP - 1, rows))

    @pl.when(t < nt - 1)
    def _():
        down.wait_send()

    @pl.when(t > 0)
    def _():
        up.wait_send()
        up2.wait_send()

    @pl.when(hub)
    def _():
        def drain(g):
            middle_copy(g).wait_send()
            for d in range(1, half_n):
                return_copy(g, d).wait_send()

        def drain_ghost(g):
            for d in range(1, half_n):
                ghost_copy(g, d).wait_send()

        repeat(groups, drain)
        repeat(pole_groups, drain_ghost)

    @pl.when(south & hub & (hub_index == second_hub))
    def _():
        for d in range(1, half_n):
            second_copy(d).wait_send()


def local(n, nt, density, velocity, bfield, levels):
    _, rows, cols, radial = density.shape
    half_n = n // 2
    groups = CHANNELS // HUBS * 2
    wide = cols + 8
    forward, back = tables(n, cols)
    any_space = pl.BlockSpec(memory_space=pl.ANY)
    vmem = pl.BlockSpec(memory_space=pltpu.VMEM)
    f32, bf16 = jnp.float32, jnp.bfloat16
    dma = pltpu.SemaphoreType.DMA
    return pl.pallas_call(
        functools.partial(kernel, n, nt, rows, cols),
        out_shape=(
            jax.ShapeDtypeStruct(density.shape, f32),
            jax.ShapeDtypeStruct(bfield.shape, f32),
        ),
        in_specs=[any_space] * 3 + [pl.BlockSpec(memory_space=pltpu.SMEM)] + [any_space] * 2,
        out_specs=(vmem, vmem),
        scratch_shapes=[
            pltpu.VMEM((CHANNELS, rows + 3, wide, radial), f32),
            pltpu.VMEM((groups, 2, half_n * cols, radial), f32),
            pltpu.VMEM((groups, 2 * KMAX, 2 * radial), f32),
            pltpu.VMEM((groups, 2 * KMAX, 2 * radial), f32),
            pltpu.VMEM((groups, 2, half_n, wide, radial), f32),
            pltpu.VMEM((groups // 2, 2, half_n, wide, radial), f32),
            pltpu.VMEM((CHANNELS * CAP, wide, radial), f32),
            pltpu.VMEM((2, 2 * KMAX, half_n * cols), bf16),
            pltpu.VMEM((2, 2, half_n * wide, 2 * KMAX), bf16),
            pltpu.VMEM((CHANNELS, rows, radial), f32),
            pltpu.VMEM((CHANNELS + 1, rows, radial), f32),
            pltpu.VMEM((CHANNELS, rows, radial), f32),
            pltpu.VMEM((CHANNELS + 1, rows, radial), f32),
            dma((6,)),
            dma((HUBS, groups)),
            dma((groups, half_n)),
            dma((groups,)),
            dma((groups,)),
            dma((groups, half_n)),
            dma((HUBS, groups)),
            dma((groups // 2, half_n)),
            dma((HUBS, groups // 2)),
            dma((half_n,)),
            dma((1,)),
            dma((2,)),
            dma((2,)),
            dma((3,)),
            dma((3,)),
        ],
        compiler_params=pltpu.CompilerParams(
            collective_id=0, has_side_effects=True, vmem_limit_bytes=60 * 1024 * 1024
        ),
        name="substep",
    )(density, velocity, bfield, levels, jnp.asarray(forward), jnp.asarray(back))


def solution(mesh):
    spec = P(None, "theta", "phi", None)
    return jax.shard_map(
        functools.partial(local, mesh.shape["phi"], mesh.shape["theta"]),
        mesh=mesh,
        in_specs=(spec, spec, spec, P()),
        out_specs=(spec, spec),
        check_vma=False,
    )
```

```python
import functools
import math

import jax
import jax.numpy as jnp
import numpy as np
import ml_dtypes
from jax import lax
from jax.experimental import pallas as pl
from jax.experimental.pallas import tpu as pltpu
from jax.sharding import PartitionSpec as P

CAP = 4
KMAX = 128
TIME_STEP = 0.2
CHANNELS = 8
HUBS = 4
ODD = (3, 4, 6, 7)
BTHETA = 6
BPHI = 7
MESH = pl.DeviceIdType.MESH


def split_table(table):
    high = table.astype(ml_dtypes.bfloat16)
    low = (table - high.astype(np.float64)).astype(ml_dtypes.bfloat16)
    return np.stack([high, low])


def tables(count, cols):
    cycle = count * cols
    orders = np.arange(KMAX)
    points = np.arange(cycle)
    angle = (orders[:, None] * points[None, :] % cycle) * (2.0 * math.pi / cycle)
    forward = np.concatenate([np.cos(angle), np.sin(angle)], axis=0)
    offset = np.concatenate([np.arange(cols + 7), [-1]])
    place = ((np.arange(count)[:, None] * cols + offset[None, :]) % cycle).reshape(-1)
    back = forward.T[place]
    return split_table(forward), split_table(back)


def flux(ql, qr, vl, vr):
    return 0.5 * (ql * vl + qr * vr) - 0.5 * jnp.maximum(jnp.abs(vl), jnp.abs(vr)) * (qr - ql)


def stencil_row(ext, dout, bout, row, rows, cols):
    wide = cols + 8
    lower = jnp.where(row == 0, rows + 2, row - 1)
    upper = row + 1
    upper2 = row + 2
    lane = lax.broadcasted_iota(jnp.int32, (wide, 128), 1)
    first = lane == 0
    last = lane == 127

    def from_left(x):
        return pltpu.roll(x, 1, 0)

    def from_right(x):
        return pltpu.roll(x, wide - 1, 0)

    def from_below(x):
        return pltpu.roll(x, 1, 1)

    def from_above(x):
        return pltpu.roll(x, 127, 1)

    vr, vt, vp = ext[2, row], ext[3, row], ext[4, row]
    vt_lo, vt_up = ext[3, lower], ext[3, upper]
    vp_l = from_left(vp)
    vr_b = jnp.where(first, vr, from_below(vr))
    for c in range(2):
        q = ext[c, row]
        tend = flux(q, ext[c, upper], vt, vt_up) - flux(ext[c, lower], q, vt_lo, vt)
        fp = flux(from_left(q), q, vp_l, vp)
        tend = tend + from_right(fp) - fp
        fr = flux(jnp.where(first, q, from_below(q)), q, vr_b, vr)
        tend = tend + jnp.where(last, q * vr, from_above(fr)) - fr
        new = q - TIME_STEP * tend
        dout[c, row] = new[:cols]

    def emfs(j, bt_next):
        ur, ut, up = ext[2, j], ext[3, j], ext[4, j]
        br, bt, bp = ext[5, j], ext[6, j], ext[7, j]
        br_c = 0.5 * (br + jnp.where(last, br, from_above(br)))
        bt_c = 0.5 * (bt + bt_next)
        bp_c = 0.5 * (bp + from_right(bp))
        e_r = -(ut * bp_c - up * bt_c)
        e_p = -(ur * bt_c - ut * br_c)
        e_p0 = -(ur * bt_c - ut * br)
        pair_p = e_p + jnp.where(first, e_p0, from_below(e_p))
        pair_r = e_r + from_left(e_r)
        return e_p, pair_p, pair_r, br_c, bp_c

    bt = ext[6, row]
    bt_up = ext[6, upper]
    ep_lo, pp_lo, pr_lo, _, _ = emfs(lower, bt)
    ep, pp, pr, br_c, bp_c = emfs(row, bt_up)
    ep_up, pp_up, pr_up, _, _ = emfs(upper, ext[6, upper2])
    br = ext[5, row]
    e_t = -(vp * br_c - vr * bp_c)
    e_t0 = -(vp * br - vr * bp_c)
    et_pair = e_t + from_left(e_t)
    et_pair0 = e_t0 + from_left(e_t0)
    edge_t = et_pair + jnp.where(first, et_pair0, from_below(et_pair))
    edge_t_above = jnp.where(last, 2.0 * et_pair, from_above(edge_t))
    edge_p = pp_lo + pp
    edge_p_above = jnp.where(last, 2.0 * (ep_lo + ep), from_above(edge_p))
    edge_r = pr_lo + pr
    scale = TIME_STEP * 0.25
    new_r = br - scale * ((pp_up - pp_lo) - (from_right(edge_t) - edge_t))
    new_t = bt - scale * ((from_right(edge_r) - edge_r) - (edge_p_above - edge_p))
    new_p = ext[7, row] - scale * ((edge_t_above - edge_t) - (pr_up - pr_lo))
    bout[0, row] = new_r[:cols]
    bout[1, row] = new_t[:cols]
    bout[2, row] = new_p[:cols]


def split(x):
    high = x.astype(jnp.bfloat16)
    return high, (x - high.astype(jnp.float32)).astype(jnp.bfloat16)


def product(table, x):
    high, low = split(x)
    dot = functools.partial(jnp.dot, preferred_element_type=jnp.float32)
    return dot(table[0], high) + (dot(table[0], low) + dot(table[1], high))


def kernel(
    n, nt, rows, cols,
    density, velocity, bfield, levels, fwd_hbm, back_hbm,
    dout, bout,
    ext, cyc, part, other_part, fil, gfil, caps, fwd, back, to_right, to_left, at_left, at_right,
    load_sem, fs, fr, ms, mr, rs, rr, gs, gr, g2s, g2r, hs, hr, ts, tr,
):
    half_n = n // 2
    groups = CHANNELS // HUBS * 2
    pole_groups = groups // 2
    wide = cols + 8
    cycle = n * cols
    t = lax.axis_index("theta")
    me = lax.axis_index("phi")
    north = t == 0
    south = t == nt - 1
    end = north | south
    cap0 = jnp.where(north, 0, rows - CAP)
    main = pl.ds(0, cols)
    half = lax.div(me, half_n)
    place = lax.rem(me, half_n)

    def hub_place(j):
        return jnp.where(half == 0, half_n - HUBS + j, j)

    hub_index = place - hub_place(0)
    hub = end & (hub_index >= 0) & (hub_index < HUBS)

    loads = [
        pltpu.make_async_copy(density, ext.at[pl.ds(0, 2), pl.ds(0, rows), main], load_sem.at[0]),
        pltpu.make_async_copy(velocity, ext.at[pl.ds(2, 3), pl.ds(0, rows), main], load_sem.at[1]),
        pltpu.make_async_copy(bfield, ext.at[pl.ds(5, 3), pl.ds(0, rows), main], load_sem.at[2]),
    ]
    width = half_n * wide
    near = pl.ds(pl.multiple_of(half * width, 16), width)
    far = pl.ds(pl.multiple_of((1 - half) * width, 16), width)
    mine = pl.ds(pl.multiple_of(half * half_n * cols, 128), half_n * cols)
    both = pl.ds(0, 2)
    modes = pl.ds(0, 2 * KMAX)
    table_loads = [
        pltpu.make_async_copy(fwd_hbm.at[both, modes, mine], fwd, load_sem.at[3]),
        pltpu.make_async_copy(back_hbm.at[both, near], back.at[0], load_sem.at[4]),
        pltpu.make_async_copy(back_hbm.at[both, far], back.at[1], load_sem.at[5]),
    ]
    for copy in loads + table_loads:
        copy.start()

    barrier = pltpu.get_barrier_semaphore()

    def other(d):
        return lax.rem(me + d, n)

    def greet(device):
        pl.semaphore_signal(barrier, inc=1, device_id=device, device_id_type=MESH)

    right, left = other(1), other(n - 1)

    @pl.when(end)
    def _():
        for d in range(1, n):
            greet({"phi": other(d)})

    @pl.when(jnp.logical_not(end))
    def _():
        greet({"phi": right})
        greet({"phi": left})

    @pl.when(t > 0)
    def _():
        greet({"theta": t - 1})

    @pl.when(t < nt - 1)
    def _():
        greet({"theta": t + 1})

    @pl.when(end)
    def _():
        pl.semaphore_wait(barrier, n)

    @pl.when(jnp.logical_not(end))
    def _():
        pl.semaphore_wait(barrier, 4)

    for copy in loads:
        copy.wait()

    def remote(src, dst, send, recv, device):
        return pltpu.make_async_remote_copy(
            src_ref=src, dst_ref=dst, send_sem=send, recv_sem=recv,
            device_id=device, device_id_type=MESH,
        )

    def await_bytes(ref, sem):
        pltpu.make_async_copy(ref, ref, sem).wait()

    def repeat(count, body):
        def step(i, carry):
            body(i)
            return carry

        lax.fori_loop(0, count, step, 0)

    def cap_pair(g):
        later = lax.div(g, pole_groups)
        return jnp.where(north, CAP - 2 - 2 * later, 2 * later)

    def channel(j, g):
        return j * pole_groups + lax.rem(g, pole_groups)

    def cap_slots(j, g):
        return pl.ds(channel(j, g) * CAP + 2 * lax.div(g, pole_groups), 2)

    def forward_copy(j, g):
        src = ext.at[channel(j, g), pl.ds(cap0 + cap_pair(g), 2), main]
        dst = cyc.at[g, both, pl.ds(pl.multiple_of(place * cols, 8), cols)]
        device = half * half_n + hub_place(j)
        return (
            pltpu.make_async_copy(src, dst, fr.at[g, place]),
            remote(src, dst, fs.at[j, g], fr.at[g, place], {"phi": device}),
        )

    def middle_copy(g):
        partner = jnp.where(half == 0, half_n, half_n - HUBS) + hub_index
        return remote(part.at[g], other_part.at[g], ms.at[g], mr.at[g], {"phi": partner})

    def target(d):
        spot = lax.rem(place + d, half_n)
        return spot, half * half_n + spot

    def return_copy(g, d):
        spot, device = target(d)
        src = fil.at[g, both, spot]
        dst = caps.at[cap_slots(hub_index, g)]
        sem = rr.at[hub_index, g]
        if d == 0:
            return pltpu.make_async_copy(src, dst, sem)
        return remote(src, dst, rs.at[g, d], sem, {"phi": device})

    ghost_row = jnp.where(north, rows + 2, rows)

    def ghost_copy(g, d):
        spot, device = target(d)
        src = gfil.at[g, jnp.where(north, 0, 1), spot]
        dst = ext.at[channel(hub_index, g), ghost_row]
        sem = gr.at[hub_index, g]
        if d == 0:
            return pltpu.make_async_copy(src, dst, sem)
        return remote(src, dst, gs.at[g, d], sem, {"phi": device})

    second_hub, second_group = BTHETA // pole_groups, BTHETA % pole_groups

    def second_copy(d):
        spot, device = target(d)
        src = gfil.at[second_group, 0, spot]
        dst = ext.at[BTHETA, rows + 1]
        if d == 0:
            return pltpu.make_async_copy(src, dst, g2r.at[0])
        return remote(src, dst, g2s.at[d], g2r.at[0], {"phi": device})

    for c in range(CHANNELS):
        to_right[c] = ext[c, 0:rows, cols - 1]
        to_left[c] = ext[c, 0:rows, 0]
    to_left[CHANNELS] = ext[BPHI, 0:rows, 1]

    go_right = remote(to_right, at_left, hs.at[0], hr.at[0], {"phi": right})
    go_left = remote(to_left, at_right, hs.at[1], hr.at[1], {"phi": left})
    go_right.start()
    go_left.start()

    @pl.when(end)
    def _():
        def send(g):
            for j in range(HUBS):
                here, away = forward_copy(j, g)

                @pl.when(hub_place(j) == place)
                def _():
                    here.start()

                @pl.when(hub_place(j) != place)
                def _():
                    away.start()

        repeat(groups, send)

    go_right.wait()
    go_left.wait()

    def unpack(lo, hi):
        for c in range(CHANNELS):
            ext[c, lo:hi, wide - 1] = at_left[c, lo:hi]
            ext[c, lo:hi, cols] = at_right[c, lo:hi]
        ext[BPHI, lo:hi, cols + 1] = at_right[CHANNELS, lo:hi]

    @pl.when(north)
    def _():
        unpack(CAP, rows)

    @pl.when(south)
    def _():
        unpack(0, rows - CAP)

    @pl.when(jnp.logical_not(end))
    def _():
        unpack(0, rows)

    every = pl.ds(0, CHANNELS)
    down = remote(ext.at[every, rows - 1], ext.at[every, rows + 2], ts.at[0], tr.at[0], {"theta": t + 1})
    up = remote(ext.at[every, 0], ext.at[every, rows], ts.at[1], tr.at[1], {"theta": t - 1})
    up2 = remote(ext.at[BTHETA, 1], ext.at[BTHETA, rows + 1], ts.at[2], tr.at[2], {"theta": t - 1})

    @pl.when(t < nt - 1)
    def _():
        down.start()

    @pl.when(t > 0)
    def _():
        up.start()
        up2.start()

    for copy in table_loads:
        copy.wait()

    @pl.when(hub)
    def _():
        pole = jnp.where(north, 0, 1)
        mode = lax.rem(lax.broadcasted_iota(jnp.int32, (2 * KMAX, 128), 0), KMAX)
        weight = jnp.where(mode == 0, 1.0 / cycle, 2.0 / cycle)

        def analyse(g):
            for i in range(half_n):
                await_bytes(cyc.at[g, both, pl.ds(i * cols, cols)], fr.at[g, i])
            part[g] = product(fwd, jnp.concatenate([cyc[g, 0], cyc[g, 1]], axis=1))
            middle_copy(g).start()

        def evaluate(g):
            await_bytes(other_part.at[g], mr.at[g])
            masks = []
            for s in range(2):
                limit = lax.shift_right_logical(jnp.int32(KMAX), levels[pole, cap_pair(g) + s])
                masks.append(jnp.where(mode < limit, weight, 0.0))
            coeffs = (part[g] + other_part[g]) * jnp.concatenate(masks, axis=1)
            values = product(back[0], coeffs)
            fil[g, 0] = values[:, :128].reshape(half_n, wide, 128)
            fil[g, 1] = values[:, 128:].reshape(half_n, wide, 128)
            for d in reversed(range(half_n)):
                return_copy(g, d).start()

            @pl.when(g >= pole_groups)
            def _():
                k = g - pole_groups
                ghosts = product(back[1], coeffs)
                gfil[k, 0] = ghosts[:, :128].reshape(half_n, wide, 128)
                gfil[k, 1] = ghosts[:, 128:].reshape(half_n, wide, 128)
                for d in reversed(range(half_n)):
                    ghost_copy(k, d).start()

        def step(g):
            @pl.when(g < groups)
            def _():
                analyse(g)

            @pl.when(g >= 1)
            def _():
                evaluate(g - 1)

        repeat(groups + 1, step)

    @pl.when(south & hub & (hub_index == second_hub))
    def _():
        for d in range(half_n):
            second_copy(d).start()

    @pl.when(t > 0)
    def _():
        down.wait_recv()

    @pl.when(t < nt - 1)
    def _():
        up.wait_recv()
        up2.wait_recv()

    def sweep(lo, hi):
        def body(row, carry):
            stencil_row(ext, dout, bout, row, rows, cols)
            return carry

        lax.fori_loop(lo, hi, body, 0)

    early_lo = jnp.where(north, CAP + 1, 0)
    early_hi = jnp.where(south, rows - CAP - 2, rows)
    sweep(early_lo, early_hi)

    @pl.when(end)
    def _():
        def sent(g):
            for j in range(HUBS):
                @pl.when(hub_place(j) != place)
                def _():
                    forward_copy(j, g)[1].wait_send()

        repeat(groups, sent)

        def take(first):
            def one(k):
                g = first + k
                for j in range(HUBS):
                    slots = cap_slots(j, g)
                    await_bytes(caps.at[slots], rr.at[j, g])
                    c = channel(j, g)
                    slot = c * CAP + 2 * lax.div(g, pole_groups)
                    r = cap0 + cap_pair(g)
                    ext[c, r] = caps[slot]
                    ext[c, r + 1] = caps[slot + 1]

            repeat(pole_groups, one)

        take(0)
        sweep(jnp.where(north, CAP - 1, rows - CAP - 2), jnp.where(north, CAP + 1, rows - CAP))
        take(pole_groups)

        def ghost(k):
            for j in range(HUBS):
                await_bytes(ext.at[channel(j, k), ghost_row], gr.at[j, k])

        repeat(pole_groups, ghost)
        for c in ODD:
            ext[c, ghost_row] = -ext[c, ghost_row]

        @pl.when(south)
        def _():
            await_bytes(ext.at[BTHETA, rows + 1], g2r.at[0])
            ext[BTHETA, rows + 1] = -ext[BTHETA, rows + 1]

        sweep(jnp.where(north, 0, rows - CAP), jnp.where(north, CAP - 1, rows))

    @pl.when(t < nt - 1)
    def _():
        down.wait_send()

    @pl.when(t > 0)
    def _():
        up.wait_send()
        up2.wait_send()

    @pl.when(hub)
    def _():
        def drain(g):
            middle_copy(g).wait_send()
            for d in range(1, half_n):
                return_copy(g, d).wait_send()

        def drain_ghost(g):
            for d in range(1, half_n):
                ghost_copy(g, d).wait_send()

        repeat(groups, drain)
        repeat(pole_groups, drain_ghost)

    @pl.when(south & hub & (hub_index == second_hub))
    def _():
        for d in range(1, half_n):
            second_copy(d).wait_send()


def local(n, nt, density, velocity, bfield, levels):
    _, rows, cols, radial = density.shape
    half_n = n // 2
    groups = CHANNELS // HUBS * 2
    wide = cols + 8
    forward, back = tables(n, cols)
    any_space = pl.BlockSpec(memory_space=pl.ANY)
    vmem = pl.BlockSpec(memory_space=pltpu.VMEM)
    f32, bf16 = jnp.float32, jnp.bfloat16
    dma = pltpu.SemaphoreType.DMA
    return pl.pallas_call(
        functools.partial(kernel, n, nt, rows, cols),
        out_shape=(
            jax.ShapeDtypeStruct(density.shape, f32),
            jax.ShapeDtypeStruct(bfield.shape, f32),
        ),
        in_specs=[any_space] * 3 + [pl.BlockSpec(memory_space=pltpu.SMEM)] + [any_space] * 2,
        out_specs=(vmem, vmem),
        scratch_shapes=[
            pltpu.VMEM((CHANNELS, rows + 3, wide, radial), f32),
            pltpu.VMEM((groups, 2, half_n * cols, radial), f32),
            pltpu.VMEM((groups, 2 * KMAX, 2 * radial), f32),
            pltpu.VMEM((groups, 2 * KMAX, 2 * radial), f32),
            pltpu.VMEM((groups, 2, half_n, wide, radial), f32),
            pltpu.VMEM((groups // 2, 2, half_n, wide, radial), f32),
            pltpu.VMEM((CHANNELS * CAP, wide, radial), f32),
            pltpu.VMEM((2, 2 * KMAX, half_n * cols), bf16),
            pltpu.VMEM((2, 2, half_n * wide, 2 * KMAX), bf16),
            pltpu.VMEM((CHANNELS, rows, radial), f32),
            pltpu.VMEM((CHANNELS + 1, rows, radial), f32),
            pltpu.VMEM((CHANNELS, rows, radial), f32),
            pltpu.VMEM((CHANNELS + 1, rows, radial), f32),
            dma((6,)),
            dma((HUBS, groups)),
            dma((groups, half_n)),
            dma((groups,)),
            dma((groups,)),
            dma((groups, half_n)),
            dma((HUBS, groups)),
            dma((groups // 2, half_n)),
            dma((HUBS, groups // 2)),
            dma((half_n,)),
            dma((1,)),
            dma((2,)),
            dma((2,)),
            dma((3,)),
            dma((3,)),
        ],
        compiler_params=pltpu.CompilerParams(
            collective_id=0, has_side_effects=True, vmem_limit_bytes=56 * 1024 * 1024
        ),
        name="substep",
    )(density, velocity, bfield, levels, jnp.asarray(forward), jnp.asarray(back))


def solution(mesh):
    spec = P(None, "theta", "phi", None)
    return jax.shard_map(
        functools.partial(local, mesh.shape["phi"], mesh.shape["theta"]),
        mesh=mesh,
        in_specs=(spec, spec, spec, P()),
        out_specs=(spec, spec),
        check_vma=False,
    )
```

```python
import functools
import math

import jax
import jax.numpy as jnp
import numpy as np
import ml_dtypes
from jax import lax
from jax.experimental import pallas as pl
from jax.experimental.pallas import tpu as pltpu
from jax.sharding import PartitionSpec as P

CAP = 4
KMAX = 128
TIME_STEP = 0.2
CHANNELS = 8
HUBS = 4
ODD = (3, 4, 6, 7)
BTHETA = 6
BPHI = 7
MESH = pl.DeviceIdType.MESH


def split_table(table):
    high = table.astype(ml_dtypes.bfloat16)
    low = (table - high.astype(np.float64)).astype(ml_dtypes.bfloat16)
    return np.stack([high, low])


def tables(count, cols):
    cycle = count * cols
    orders = np.arange(KMAX)
    points = np.arange(cycle)
    angle = (orders[:, None] * points[None, :] % cycle) * (2.0 * math.pi / cycle)
    forward = np.concatenate([np.cos(angle), np.sin(angle)], axis=0)
    offset = np.concatenate([np.arange(cols + 7), [-1]])
    place = ((np.arange(count)[:, None] * cols + offset[None, :]) % cycle).reshape(-1)
    back = forward.T[place]
    return split_table(forward), split_table(back)


def roll_left(x):
    return pltpu.roll(x, 1, 0)


def roll_right(x):
    return pltpu.roll(x, x.shape[0] - 1, 0)


def roll_below(x):
    return pltpu.roll(x, 1, 1)


def roll_above(x):
    return pltpu.roll(x, x.shape[1] - 1, 1)


def lanes(cols):
    lane = lax.broadcasted_iota(jnp.int32, (cols + 8, 128), 1)
    return lane == 0, lane == 127


def emf_row(ext, emf, j, rows, cols):
    first, last = lanes(cols)
    at = jnp.where(j < 0, rows + 2, j)
    ur, ut, up = ext[2, at], ext[3, at], ext[4, at]
    br, bt, bp = ext[5, at], ext[6, at], ext[7, at]
    bt_s = bt + ext[6, j + 1]
    br_s = br + jnp.where(last, br, roll_above(br))
    e_p = ut * br_s - ur * bt_s
    emf[0, j + 1] = e_p
    e_p0 = ut * (br + br) - ur * bt_s
    emf[1, j + 1] = e_p + jnp.where(first, e_p0, roll_below(e_p))
    e_r = up * bt_s - ut * (bp + roll_right(bp))
    emf[2, j + 1] = e_r + roll_left(e_r)


def flux_weights(hl, hr):
    most = jnp.maximum(jnp.abs(hl), jnp.abs(hr))
    return hl + most, hr - most


def stencil_row(ext, emf, dout, bout, row, rows, cols):
    first, last = lanes(cols)
    lower = jnp.where(row == 0, rows + 2, row - 1)
    upper = row + 1

    vr, vp = ext[2, row], ext[4, row]
    ht = 0.5 * ext[3, row]
    lo_l, lo_r = flux_weights(0.5 * ext[3, lower], ht)
    up_l, up_r = flux_weights(ht, 0.5 * ext[3, upper])
    middle = up_l - lo_r
    hp = 0.5 * vp
    p_l, p_r = flux_weights(roll_left(hp), hp)
    hr = 0.5 * vr
    r_l, r_r = flux_weights(jnp.where(first, hr, roll_below(hr)), hr)
    for c in range(2):
        q = ext[c, row]
        tend = middle * q + (up_r * ext[c, upper] - lo_l * ext[c, lower])
        fp = p_l * roll_left(q) + p_r * q
        fr = r_l * jnp.where(first, q, roll_below(q)) + r_r * q
        tend = tend + (roll_right(fp) - fp)
        tend = tend + (jnp.where(last, q * vr, roll_above(fr)) - fr)
        dout[c, row] = (q - TIME_STEP * tend)[:cols]

    br, bp = ext[5, row], ext[7, row]
    bp_s = bp + roll_right(bp)
    br_s = br + jnp.where(last, br, roll_above(br))
    vr_bp = vr * bp_s
    e_t = vr_bp - vp * br_s
    e_t0 = vr_bp - vp * (br + br)
    pair = e_t + roll_left(e_t)
    pair0 = e_t0 + roll_left(e_t0)
    edge_t = pair + jnp.where(first, pair0, roll_below(pair))
    scale = TIME_STEP * 0.125
    new_r = br - scale * (
        (emf[1, row + 2] - emf[1, row]) - (roll_right(edge_t) - edge_t)
    )
    bout[0, row] = new_r[:cols]
    edge_t_above = jnp.where(last, 2.0 * pair, roll_above(edge_t))
    new_p = bp - scale * ((edge_t_above - edge_t) - (emf[2, row + 2] - emf[2, row]))
    bout[2, row] = new_p[:cols]
    edge_p = emf[1, row] + emf[1, row + 1]
    edge_p_above = jnp.where(last, 2.0 * (emf[0, row] + emf[0, row + 1]), roll_above(edge_p))
    edge_r = emf[2, row] + emf[2, row + 1]
    new_t = ext[6, row] - scale * (
        (roll_right(edge_r) - edge_r) - (edge_p_above - edge_p)
    )
    bout[1, row] = new_t[:cols]


def split(x):
    high = x.astype(jnp.bfloat16)
    return high, (x - high.astype(jnp.float32)).astype(jnp.bfloat16)


def product(table, x):
    high, low = split(x)
    dot = functools.partial(jnp.dot, preferred_element_type=jnp.float32)
    return dot(table[0], high) + (dot(table[0], low) + dot(table[1], high))


def kernel(
    n, nt, rows, cols,
    density, velocity, bfield, levels, fwd_hbm, back_hbm,
    dout, bout,
    ext, emf, cyc, part, other_part, fil, gfil, caps, fwd, back, to_right, to_left, at_left, at_right,
    load_sem, fs, fr, ms, mr, rs, rr, gs, gr, g2s, g2r, hs, hr, ts, tr,
):
    half_n = n // 2
    groups = CHANNELS // HUBS * 2
    pole_groups = groups // 2
    wide = cols + 8
    cycle = n * cols
    t = lax.axis_index("theta")
    me = lax.axis_index("phi")
    north = t == 0
    south = t == nt - 1
    end = north | south
    cap0 = jnp.where(north, 0, rows - CAP)
    main = pl.ds(0, cols)
    half = lax.div(me, half_n)
    place = lax.rem(me, half_n)

    def hub_place(j):
        return jnp.where(half == 0, half_n - HUBS + j, j)

    hub_index = place - hub_place(0)
    hub = end & (hub_index >= 0) & (hub_index < HUBS)

    loads = [
        pltpu.make_async_copy(density, ext.at[pl.ds(0, 2), pl.ds(0, rows), main], load_sem.at[0]),
        pltpu.make_async_copy(velocity, ext.at[pl.ds(2, 3), pl.ds(0, rows), main], load_sem.at[1]),
        pltpu.make_async_copy(bfield, ext.at[pl.ds(5, 3), pl.ds(0, rows), main], load_sem.at[2]),
    ]
    width = half_n * wide
    near = pl.ds(pl.multiple_of(half * width, 16), width)
    far = pl.ds(pl.multiple_of((1 - half) * width, 16), width)
    mine = pl.ds(pl.multiple_of(half * half_n * cols, 128), half_n * cols)
    both = pl.ds(0, 2)
    modes = pl.ds(0, 2 * KMAX)
    table_loads = [
        pltpu.make_async_copy(fwd_hbm.at[both, modes, mine], fwd, load_sem.at[3]),
        pltpu.make_async_copy(back_hbm.at[both, near], back.at[0], load_sem.at[4]),
        pltpu.make_async_copy(back_hbm.at[both, far], back.at[1], load_sem.at[5]),
    ]
    for copy in loads + table_loads:
        copy.start()

    barrier = pltpu.get_barrier_semaphore()

    def other(d):
        return lax.rem(me + d, n)

    def greet(device):
        pl.semaphore_signal(barrier, inc=1, device_id=device, device_id_type=MESH)

    right, left = other(1), other(n - 1)

    @pl.when(end)
    def _():
        for d in range(1, n):
            greet({"phi": other(d)})

    @pl.when(jnp.logical_not(end))
    def _():
        greet({"phi": right})
        greet({"phi": left})

    @pl.when(t > 0)
    def _():
        greet({"theta": t - 1})

    @pl.when(t < nt - 1)
    def _():
        greet({"theta": t + 1})

    @pl.when(end)
    def _():
        pl.semaphore_wait(barrier, n)

    @pl.when(jnp.logical_not(end))
    def _():
        pl.semaphore_wait(barrier, 4)

    for copy in loads:
        copy.wait()

    def remote(src, dst, send, recv, device):
        return pltpu.make_async_remote_copy(
            src_ref=src, dst_ref=dst, send_sem=send, recv_sem=recv,
            device_id=device, device_id_type=MESH,
        )

    def await_bytes(ref, sem):
        pltpu.make_async_copy(ref, ref, sem).wait()

    def repeat(count, body):
        def step(i, carry):
            body(i)
            return carry

        lax.fori_loop(0, count, step, 0)

    def cap_pair(g):
        later = lax.div(g, pole_groups)
        return jnp.where(north, CAP - 2 - 2 * later, 2 * later)

    def channel(j, g):
        return j * pole_groups + lax.rem(g, pole_groups)

    def cap_slots(j, g):
        return pl.ds(channel(j, g) * CAP + 2 * lax.div(g, pole_groups), 2)

    def forward_copy(j, g):
        src = ext.at[channel(j, g), pl.ds(cap0 + cap_pair(g), 2), main]
        dst = cyc.at[g, both, pl.ds(pl.multiple_of(place * cols, 8), cols)]
        device = half * half_n + hub_place(j)
        return (
            pltpu.make_async_copy(src, dst, fr.at[g, place]),
            remote(src, dst, fs.at[j, g], fr.at[g, place], {"phi": device}),
        )

    def middle_copy(g):
        partner = jnp.where(half == 0, half_n, half_n - HUBS) + hub_index
        return remote(part.at[g], other_part.at[g], ms.at[g], mr.at[g], {"phi": partner})

    def target(d):
        spot = lax.rem(place + d, half_n)
        return spot, half * half_n + spot

    def return_copy(g, d):
        spot, device = target(d)
        src = fil.at[g, both, spot]
        dst = caps.at[cap_slots(hub_index, g)]
        sem = rr.at[hub_index, g]
        if d == 0:
            return pltpu.make_async_copy(src, dst, sem)
        return remote(src, dst, rs.at[g, d], sem, {"phi": device})

    ghost_row = jnp.where(north, rows + 2, rows)

    def ghost_copy(g, d):
        spot, device = target(d)
        src = gfil.at[g, jnp.where(north, 0, 1), spot]
        dst = ext.at[channel(hub_index, g), ghost_row]
        sem = gr.at[hub_index, g]
        if d == 0:
            return pltpu.make_async_copy(src, dst, sem)
        return remote(src, dst, gs.at[g, d], sem, {"phi": device})

    second_hub, second_group = BTHETA // pole_groups, BTHETA % pole_groups

    def second_copy(d):
        spot, device = target(d)
        src = gfil.at[second_group, 0, spot]
        dst = ext.at[BTHETA, rows + 1]
        if d == 0:
            return pltpu.make_async_copy(src, dst, g2r.at[0])
        return remote(src, dst, g2s.at[d], g2r.at[0], {"phi": device})

    for c in range(CHANNELS):
        to_right[c] = ext[c, 0:rows, cols - 1]
        to_left[c] = ext[c, 0:rows, 0]
    to_left[CHANNELS] = ext[BPHI, 0:rows, 1]

    go_right = remote(to_right, at_left, hs.at[0], hr.at[0], {"phi": right})
    go_left = remote(to_left, at_right, hs.at[1], hr.at[1], {"phi": left})
    go_right.start()
    go_left.start()

    @pl.when(end)
    def _():
        def send(g):
            for j in range(HUBS):
                here, away = forward_copy(j, g)

                @pl.when(hub_place(j) == place)
                def _():
                    here.start()

                @pl.when(hub_place(j) != place)
                def _():
                    away.start()

        repeat(groups, send)

    go_right.wait()
    go_left.wait()

    def unpack(lo, hi):
        for c in range(CHANNELS):
            ext[c, lo:hi, wide - 1] = at_left[c, lo:hi]
            ext[c, lo:hi, cols] = at_right[c, lo:hi]
        ext[BPHI, lo:hi, cols + 1] = at_right[CHANNELS, lo:hi]

    @pl.when(north)
    def _():
        unpack(CAP, rows)

    @pl.when(south)
    def _():
        unpack(0, rows - CAP)

    @pl.when(jnp.logical_not(end))
    def _():
        unpack(0, rows)

    every = pl.ds(0, CHANNELS)
    down = remote(ext.at[every, rows - 1], ext.at[every, rows + 2], ts.at[0], tr.at[0], {"theta": t + 1})
    up = remote(ext.at[every, 0], ext.at[every, rows], ts.at[1], tr.at[1], {"theta": t - 1})
    up2 = remote(ext.at[BTHETA, 1], ext.at[BTHETA, rows + 1], ts.at[2], tr.at[2], {"theta": t - 1})

    @pl.when(t < nt - 1)
    def _():
        down.start()

    @pl.when(t > 0)
    def _():
        up.start()
        up2.start()

    for copy in table_loads:
        copy.wait()

    def sweep(lo, hi):
        def body(row, carry):
            stencil_row(ext, emf, dout, bout, row, rows, cols)
            return carry

        lax.fori_loop(lo, hi, body, 0)

    def make_emfs(lo, hi):
        def body(j, carry):
            emf_row(ext, emf, j, rows, cols)
            return carry

        lax.fori_loop(lo, hi, body, 0)

    early_lo = jnp.where(north, CAP + 1, 0)
    early_hi = jnp.where(south, rows - CAP - 2, rows)

    def ready():
        @pl.when(t > 0)
        def _():
            down.wait_recv()

        @pl.when(t < nt - 1)
        def _():
            up.wait_recv()
            up2.wait_recv()

        make_emfs(jnp.where(north, CAP, -1), jnp.where(south, rows - CAP - 1, rows + 1))

    @pl.when(hub)
    def _():
        pole = jnp.where(north, 0, 1)
        mode = lax.rem(lax.broadcasted_iota(jnp.int32, (2 * KMAX, 128), 0), KMAX)
        weight = jnp.where(mode == 0, 1.0 / cycle, 2.0 / cycle)

        def analyse(g):
            for i in range(half_n):
                await_bytes(cyc.at[g, both, pl.ds(i * cols, cols)], fr.at[g, i])
            part[g] = product(fwd, jnp.concatenate([cyc[g, 0], cyc[g, 1]], axis=1))
            middle_copy(g).start()

        def evaluate(g):
            await_bytes(other_part.at[g], mr.at[g])
            masks = []
            for s in range(2):
                limit = lax.shift_right_logical(jnp.int32(KMAX), levels[pole, cap_pair(g) + s])
                masks.append(jnp.where(mode < limit, weight, 0.0))
            coeffs = (part[g] + other_part[g]) * jnp.concatenate(masks, axis=1)
            values = product(back[0], coeffs)
            fil[g, 0] = values[:, :128].reshape(half_n, wide, 128)
            fil[g, 1] = values[:, 128:].reshape(half_n, wide, 128)
            for d in reversed(range(half_n)):
                return_copy(g, d).start()

            @pl.when(g >= pole_groups)
            def _():
                k = g - pole_groups
                ghosts = product(back[1], coeffs)
                gfil[k, 0] = ghosts[:, :128].reshape(half_n, wide, 128)
                gfil[k, 1] = ghosts[:, 128:].reshape(half_n, wide, 128)
                for d in reversed(range(half_n)):
                    ghost_copy(k, d).start()

        def step(g):
            @pl.when(g < groups)
            def _():
                analyse(g)

            @pl.when(g == 1)
            def _():
                ready()

            @pl.when(g >= 1)
            def _():
                row = early_lo + g - 1
                sweep(row, jnp.minimum(row + 1, early_hi))
                evaluate(g - 1)

        repeat(groups + 1, step)
        sweep(early_lo + groups, early_hi)

    @pl.when(south & hub & (hub_index == second_hub))
    def _():
        for d in range(half_n):
            second_copy(d).start()

    @pl.when(jnp.logical_not(hub))
    def _():
        ready()
        sweep(early_lo, early_hi)

    @pl.when(end)
    def _():
        def sent(g):
            for j in range(HUBS):
                @pl.when(hub_place(j) != place)
                def _():
                    forward_copy(j, g)[1].wait_send()

        repeat(groups, sent)

        def take(first):
            def one(k):
                g = first + k
                for j in range(HUBS):
                    slots = cap_slots(j, g)
                    await_bytes(caps.at[slots], rr.at[j, g])
                    c = channel(j, g)
                    slot = c * CAP + 2 * lax.div(g, pole_groups)
                    r = cap0 + cap_pair(g)
                    ext[c, r] = caps[slot]
                    ext[c, r + 1] = caps[slot + 1]

            repeat(pole_groups, one)

        take(0)
        make_emfs(
            jnp.where(north, CAP - 2, rows - CAP - 1), jnp.where(north, CAP, rows - CAP + 1)
        )
        sweep(jnp.where(north, CAP - 1, rows - CAP - 2), jnp.where(north, CAP + 1, rows - CAP))
        take(pole_groups)

        def ghost(k):
            for j in range(HUBS):
                await_bytes(ext.at[channel(j, k), ghost_row], gr.at[j, k])

        repeat(pole_groups, ghost)
        for c in ODD:
            ext[c, ghost_row] = -ext[c, ghost_row]

        @pl.when(south)
        def _():
            await_bytes(ext.at[BTHETA, rows + 1], g2r.at[0])
            ext[BTHETA, rows + 1] = -ext[BTHETA, rows + 1]

        make_emfs(jnp.where(north, -1, rows - CAP + 1), jnp.where(north, CAP - 2, rows + 1))
        sweep(jnp.where(north, 0, rows - CAP), jnp.where(north, CAP - 1, rows))

    @pl.when(t < nt - 1)
    def _():
        down.wait_send()

    @pl.when(t > 0)
    def _():
        up.wait_send()
        up2.wait_send()

    @pl.when(hub)
    def _():
        def drain(g):
            middle_copy(g).wait_send()
            for d in range(1, half_n):
                return_copy(g, d).wait_send()

        def drain_ghost(g):
            for d in range(1, half_n):
                ghost_copy(g, d).wait_send()

        repeat(groups, drain)
        repeat(pole_groups, drain_ghost)

    @pl.when(south & hub & (hub_index == second_hub))
    def _():
        for d in range(1, half_n):
            second_copy(d).wait_send()


def local(n, nt, density, velocity, bfield, levels):
    _, rows, cols, radial = density.shape
    half_n = n // 2
    groups = CHANNELS // HUBS * 2
    wide = cols + 8
    forward, back = tables(n, cols)
    any_space = pl.BlockSpec(memory_space=pl.ANY)
    vmem = pl.BlockSpec(memory_space=pltpu.VMEM)
    f32, bf16 = jnp.float32, jnp.bfloat16
    dma = pltpu.SemaphoreType.DMA
    return pl.pallas_call(
        functools.partial(kernel, n, nt, rows, cols),
        out_shape=(
            jax.ShapeDtypeStruct(density.shape, f32),
            jax.ShapeDtypeStruct(bfield.shape, f32),
        ),
        in_specs=[any_space] * 3 + [pl.BlockSpec(memory_space=pltpu.SMEM)] + [any_space] * 2,
        out_specs=(vmem, vmem),
        scratch_shapes=[
            pltpu.VMEM((CHANNELS, rows + 3, wide, radial), f32),
            pltpu.VMEM((3, rows + 2, wide, radial), f32),
            pltpu.VMEM((groups, 2, half_n * cols, radial), f32),
            pltpu.VMEM((groups, 2 * KMAX, 2 * radial), f32),
            pltpu.VMEM((groups, 2 * KMAX, 2 * radial), f32),
            pltpu.VMEM((groups, 2, half_n, wide, radial), f32),
            pltpu.VMEM((groups // 2, 2, half_n, wide, radial), f32),
            pltpu.VMEM((CHANNELS * CAP, wide, radial), f32),
            pltpu.VMEM((2, 2 * KMAX, half_n * cols), bf16),
            pltpu.VMEM((2, 2, half_n * wide, 2 * KMAX), bf16),
            pltpu.VMEM((CHANNELS, rows, radial), f32),
            pltpu.VMEM((CHANNELS + 1, rows, radial), f32),
            pltpu.VMEM((CHANNELS, rows, radial), f32),
            pltpu.VMEM((CHANNELS + 1, rows, radial), f32),
            dma((6,)),
            dma((HUBS, groups)),
            dma((groups, half_n)),
            dma((groups,)),
            dma((groups,)),
            dma((groups, half_n)),
            dma((HUBS, groups)),
            dma((groups // 2, half_n)),
            dma((HUBS, groups // 2)),
            dma((half_n,)),
            dma((1,)),
            dma((2,)),
            dma((2,)),
            dma((3,)),
            dma((3,)),
        ],
        compiler_params=pltpu.CompilerParams(
            collective_id=0, has_side_effects=True, vmem_limit_bytes=56 * 1024 * 1024
        ),
        name="substep",
    )(density, velocity, bfield, levels, jnp.asarray(forward), jnp.asarray(back))


def solution(mesh):
    spec = P(None, "theta", "phi", None)
    return jax.shard_map(
        functools.partial(local, mesh.shape["phi"], mesh.shape["theta"]),
        mesh=mesh,
        in_specs=(spec, spec, spec, P()),
        out_specs=(spec, spec),
        check_vma=False,
    )
```

```python
import functools
import math

import jax
import jax.numpy as jnp
import numpy as np
import ml_dtypes
from jax import lax
from jax.experimental import pallas as pl
from jax.experimental.pallas import tpu as pltpu
from jax.sharding import PartitionSpec as P

CAP = 4
KMAX = 128
TIME_STEP = 0.2
CHANNELS = 8
HUBS = 4
SHARE = (1, 1, 3, 3)
BASE = (0, 1, 2, 5)
ODD = (3, 4, 6, 7)
BTHETA = 6
BPHI = 7
MESH = pl.DeviceIdType.MESH


def split_table(table):
    high = table.astype(ml_dtypes.bfloat16)
    low = (table - high.astype(np.float64)).astype(ml_dtypes.bfloat16)
    return np.stack([high, low])


def tables(count, cols):
    cycle = count * cols
    orders = np.arange(KMAX)
    points = np.arange(cycle)
    angle = (orders[:, None] * points[None, :] % cycle) * (2.0 * math.pi / cycle)
    forward = np.concatenate([np.cos(angle), np.sin(angle)], axis=0)
    offset = np.concatenate([np.arange(cols + 7), [-1]])
    place = ((np.arange(count)[:, None] * cols + offset[None, :]) % cycle).reshape(-1)
    back = forward.T[place]
    return split_table(forward), split_table(back)


def roll_left(x):
    return pltpu.roll(x, 1, 0)


def roll_right(x):
    return pltpu.roll(x, x.shape[0] - 1, 0)


def roll_below(x):
    return pltpu.roll(x, 1, 1)


def roll_above(x):
    return pltpu.roll(x, x.shape[1] - 1, 1)


def lanes(cols):
    lane = lax.broadcasted_iota(jnp.int32, (cols + 8, 128), 1)
    return lane == 0, lane == 127


def emf_row(ext, emf, j, rows, cols):
    first, last = lanes(cols)
    at = jnp.where(j < 0, rows + 2, j)
    ur, ut, up = ext[2, at], ext[3, at], ext[4, at]
    br, bt, bp = ext[5, at], ext[6, at], ext[7, at]
    bt_s = bt + ext[6, j + 1]
    br_s = br + jnp.where(last, br, roll_above(br))
    e_p = ut * br_s - ur * bt_s
    emf[0, j + 1] = e_p
    e_p0 = ut * (br + br) - ur * bt_s
    emf[1, j + 1] = e_p + jnp.where(first, e_p0, roll_below(e_p))
    e_r = up * bt_s - ut * (bp + roll_right(bp))
    emf[2, j + 1] = e_r + roll_left(e_r)


def flux_weights(hl, hr):
    most = jnp.maximum(jnp.abs(hl), jnp.abs(hr))
    return hl + most, hr - most


def stencil_row(ext, emf, dout, bout, row, rows, cols):
    first, last = lanes(cols)
    lower = jnp.where(row == 0, rows + 2, row - 1)
    upper = row + 1

    vr, vp = ext[2, row], ext[4, row]
    ht = 0.5 * ext[3, row]
    lo_l, lo_r = flux_weights(0.5 * ext[3, lower], ht)
    up_l, up_r = flux_weights(ht, 0.5 * ext[3, upper])
    middle = up_l - lo_r
    hp = 0.5 * vp
    p_l, p_r = flux_weights(roll_left(hp), hp)
    hr = 0.5 * vr
    r_l, r_r = flux_weights(jnp.where(first, hr, roll_below(hr)), hr)
    for c in range(2):
        q = ext[c, row]
        tend = middle * q + (up_r * ext[c, upper] - lo_l * ext[c, lower])
        fp = p_l * roll_left(q) + p_r * q
        fr = r_l * jnp.where(first, q, roll_below(q)) + r_r * q
        tend = tend + (roll_right(fp) - fp)
        tend = tend + (jnp.where(last, q * vr, roll_above(fr)) - fr)
        dout[c, row] = (q - TIME_STEP * tend)[:cols]

    br, bp = ext[5, row], ext[7, row]
    bp_s = bp + roll_right(bp)
    br_s = br + jnp.where(last, br, roll_above(br))
    vr_bp = vr * bp_s
    e_t = vr_bp - vp * br_s
    e_t0 = vr_bp - vp * (br + br)
    pair = e_t + roll_left(e_t)
    pair0 = e_t0 + roll_left(e_t0)
    edge_t = pair + jnp.where(first, pair0, roll_below(pair))
    scale = TIME_STEP * 0.125
    new_r = br - scale * (
        (emf[1, row + 2] - emf[1, row]) - (roll_right(edge_t) - edge_t)
    )
    bout[0, row] = new_r[:cols]
    edge_t_above = jnp.where(last, 2.0 * pair, roll_above(edge_t))
    new_p = bp - scale * ((edge_t_above - edge_t) - (emf[2, row + 2] - emf[2, row]))
    bout[2, row] = new_p[:cols]
    edge_p = emf[1, row] + emf[1, row + 1]
    edge_p_above = jnp.where(last, 2.0 * (emf[0, row] + emf[0, row + 1]), roll_above(edge_p))
    edge_r = emf[2, row] + emf[2, row + 1]
    new_t = ext[6, row] - scale * (
        (roll_right(edge_r) - edge_r) - (edge_p_above - edge_p)
    )
    bout[1, row] = new_t[:cols]


def split(x):
    high = x.astype(jnp.bfloat16)
    return high, (x - high.astype(jnp.float32)).astype(jnp.bfloat16)


def product(table, x):
    high, low = split(x)
    dot = functools.partial(jnp.dot, preferred_element_type=jnp.float32)
    return dot(table[0], high) + (dot(table[0], low) + dot(table[1], high))


def kernel(
    n, nt, rows, cols,
    density, velocity, bfield, levels, fwd_hbm, back_hbm,
    dout, bout,
    ext, emf, cyc, part, other_part, fil, gfil, caps, fwd, back, to_right, to_left, at_left, at_right,
    load_sem, fs, fr, ms, mr, rs, rr, gs, gr, g2s, g2r, hs, hr, ts, tr,
):
    half_n = n // 2
    wide = cols + 8
    cycle = n * cols
    t = lax.axis_index("theta")
    me = lax.axis_index("phi")
    north = t == 0
    south = t == nt - 1
    end = north | south
    cap0 = jnp.where(north, 0, rows - CAP)
    main = pl.ds(0, cols)
    half = lax.div(me, half_n)
    place = lax.rem(me, half_n)

    def hub_place(j):
        return jnp.where(half == 0, half_n - HUBS + j, (j + 2) % HUBS)

    hub = end & jnp.where(half == 0, place >= half_n - HUBS, place < HUBS)
    hub_index = jnp.where(half == 0, place - (half_n - HUBS), lax.rem(place + 2, HUBS))

    def share(j):
        return SHARE[j] if isinstance(j, int) else jnp.where(j < 2, 1, 3)

    def base(j):
        return BASE[j] if isinstance(j, int) else jnp.where(j < 2, j, 3 * j - 4)

    my_share = share(hub_index)

    loads = [
        pltpu.make_async_copy(density, ext.at[pl.ds(0, 2), pl.ds(0, rows), main], load_sem.at[0]),
        pltpu.make_async_copy(velocity, ext.at[pl.ds(2, 3), pl.ds(0, rows), main], load_sem.at[1]),
        pltpu.make_async_copy(bfield, ext.at[pl.ds(5, 3), pl.ds(0, rows), main], load_sem.at[2]),
    ]
    width = half_n * wide
    near = pl.ds(pl.multiple_of(half * width, 16), width)
    far = pl.ds(pl.multiple_of((1 - half) * width, 16), width)
    mine = pl.ds(pl.multiple_of(half * half_n * cols, 128), half_n * cols)
    both = pl.ds(0, 2)
    modes = pl.ds(0, 2 * KMAX)
    table_loads = [
        pltpu.make_async_copy(fwd_hbm.at[both, modes, mine], fwd, load_sem.at[3]),
        pltpu.make_async_copy(back_hbm.at[both, near], back.at[0], load_sem.at[4]),
        pltpu.make_async_copy(back_hbm.at[both, far], back.at[1], load_sem.at[5]),
    ]
    for copy in loads + table_loads:
        copy.start()

    barrier = pltpu.get_barrier_semaphore()

    def other(d):
        return lax.rem(me + d, n)

    def greet(device):
        pl.semaphore_signal(barrier, inc=1, device_id=device, device_id_type=MESH)

    right, left = other(1), other(n - 1)

    @pl.when(end)
    def _():
        for d in range(1, n):
            greet({"phi": other(d)})

    @pl.when(jnp.logical_not(end))
    def _():
        greet({"phi": right})
        greet({"phi": left})

    @pl.when(t > 0)
    def _():
        greet({"theta": t - 1})

    @pl.when(t < nt - 1)
    def _():
        greet({"theta": t + 1})

    @pl.when(end)
    def _():
        pl.semaphore_wait(barrier, n)

    @pl.when(jnp.logical_not(end))
    def _():
        pl.semaphore_wait(barrier, 4)

    for copy in loads:
        copy.wait()

    def remote(src, dst, send, recv, device):
        return pltpu.make_async_remote_copy(
            src_ref=src, dst_ref=dst, send_sem=send, recv_sem=recv,
            device_id=device, device_id_type=MESH,
        )

    def await_bytes(ref, sem):
        pltpu.make_async_copy(ref, ref, sem).wait()

    def repeat(count, body):
        def step(i, carry):
            body(i)
            return carry

        lax.fori_loop(0, count, step, 0)

    def cap_pair(j, g):
        later = lax.div(g, share(j))
        return jnp.where(north, CAP - 2 - 2 * later, 2 * later)

    def channel(j, g):
        return base(j) + lax.rem(g, share(j))

    def cap_slots(j, g):
        return pl.ds(channel(j, g) * CAP + 2 * lax.div(g, share(j)), 2)

    def forward_copy(j, g):
        src = ext.at[channel(j, g), pl.ds(cap0 + cap_pair(j, g), 2), main]
        dst = cyc.at[g, both, pl.ds(pl.multiple_of(place * cols, 8), cols)]
        device = half * half_n + hub_place(j)
        return (
            pltpu.make_async_copy(src, dst, fr.at[g, place]),
            remote(src, dst, fs.at[j, g], fr.at[g, place], {"phi": device}),
        )

    def middle_copy(g):
        partner = jnp.where(half == 0, half_n + lax.rem(hub_index + 2, HUBS), half_n - HUBS + hub_index)
        return remote(part.at[g], other_part.at[g], ms.at[g], mr.at[g], {"phi": partner})

    def target(d):
        spot = lax.rem(place + d, half_n)
        return spot, half * half_n + spot

    def return_copy(g, d):
        spot, device = target(d)
        src = fil.at[g, both, spot]
        dst = caps.at[cap_slots(hub_index, g)]
        sem = rr.at[hub_index, g]
        if d == 0:
            return pltpu.make_async_copy(src, dst, sem)
        return remote(src, dst, rs.at[g, d], sem, {"phi": device})

    ghost_row = jnp.where(north, rows + 2, rows)

    def ghost_copy(g, d):
        spot, device = target(d)
        src = gfil.at[g, jnp.where(north, 0, 1), spot]
        dst = ext.at[channel(hub_index, g), ghost_row]
        sem = gr.at[hub_index, g]
        if d == 0:
            return pltpu.make_async_copy(src, dst, sem)
        return remote(src, dst, gs.at[g, d], sem, {"phi": device})

    second_hub, second_group = HUBS - 1, BTHETA - BASE[HUBS - 1]

    def second_copy(d):
        spot, device = target(d)
        src = gfil.at[second_group, 0, spot]
        dst = ext.at[BTHETA, rows + 1]
        if d == 0:
            return pltpu.make_async_copy(src, dst, g2r.at[0])
        return remote(src, dst, g2s.at[d], g2r.at[0], {"phi": device})

    for c in range(CHANNELS):
        to_right[c] = ext[c, 0:rows, cols - 1]
        to_left[c] = ext[c, 0:rows, 0]
    to_left[CHANNELS] = ext[BPHI, 0:rows, 1]

    go_right = remote(to_right, at_left, hs.at[0], hr.at[0], {"phi": right})
    go_left = remote(to_left, at_right, hs.at[1], hr.at[1], {"phi": left})
    go_right.start()
    go_left.start()

    @pl.when(end)
    def _():
        def send(g):
            for j in reversed(range(HUBS)):
                here, away = forward_copy(j, g)
                due = g < 2 * SHARE[j]

                @pl.when(due & (hub_place(j) == place))
                def _():
                    here.start()

                @pl.when(due & (hub_place(j) != place))
                def _():
                    away.start()

        repeat(2 * max(SHARE), send)

    go_right.wait()
    go_left.wait()

    def unpack(lo, hi):
        for c in range(CHANNELS):
            ext[c, lo:hi, wide - 1] = at_left[c, lo:hi]
            ext[c, lo:hi, cols] = at_right[c, lo:hi]
        ext[BPHI, lo:hi, cols + 1] = at_right[CHANNELS, lo:hi]

    @pl.when(north)
    def _():
        unpack(CAP, rows)

    @pl.when(south)
    def _():
        unpack(0, rows - CAP)

    @pl.when(jnp.logical_not(end))
    def _():
        unpack(0, rows)

    every = pl.ds(0, CHANNELS)
    down = remote(ext.at[every, rows - 1], ext.at[every, rows + 2], ts.at[0], tr.at[0], {"theta": t + 1})
    up = remote(ext.at[every, 0], ext.at[every, rows], ts.at[1], tr.at[1], {"theta": t - 1})
    up2 = remote(ext.at[BTHETA, 1], ext.at[BTHETA, rows + 1], ts.at[2], tr.at[2], {"theta": t - 1})

    @pl.when(t < nt - 1)
    def _():
        down.start()

    @pl.when(t > 0)
    def _():
        up.start()
        up2.start()

    for copy in table_loads:
        copy.wait()

    def sweep(lo, hi):
        def body(row, carry):
            stencil_row(ext, emf, dout, bout, row, rows, cols)
            return carry

        lax.fori_loop(lo, hi, body, 0)

    def make_emfs(lo, hi):
        def body(j, carry):
            emf_row(ext, emf, j, rows, cols)
            return carry

        lax.fori_loop(lo, hi, body, 0)

    early_lo = jnp.where(north, CAP + 1, 0)
    early_hi = jnp.where(south, rows - CAP - 2, rows)

    def ready():
        @pl.when(t > 0)
        def _():
            down.wait_recv()

        @pl.when(t < nt - 1)
        def _():
            up.wait_recv()
            up2.wait_recv()

        make_emfs(jnp.where(north, CAP, -1), jnp.where(south, rows - CAP - 1, rows + 1))

    @pl.when(hub)
    def _():
        pole = jnp.where(north, 0, 1)
        mode = lax.rem(lax.broadcasted_iota(jnp.int32, (2 * KMAX, 128), 0), KMAX)
        weight = jnp.where(mode == 0, 1.0 / cycle, 2.0 / cycle)

        def analyse(g):
            for i in range(half_n):
                await_bytes(cyc.at[g, both, pl.ds(i * cols, cols)], fr.at[g, i])
            part[g] = product(fwd, jnp.concatenate([cyc[g, 0], cyc[g, 1]], axis=1))
            middle_copy(g).start()

        def evaluate(g):
            await_bytes(other_part.at[g], mr.at[g])
            masks = []
            for s in range(2):
                limit = lax.shift_right_logical(jnp.int32(KMAX), levels[pole, cap_pair(hub_index, g) + s])
                masks.append(jnp.where(mode < limit, weight, 0.0))
            coeffs = (part[g] + other_part[g]) * jnp.concatenate(masks, axis=1)
            values = product(back[0], coeffs)
            fil[g, 0] = values[:, :128].reshape(half_n, wide, 128)
            fil[g, 1] = values[:, 128:].reshape(half_n, wide, 128)
            for d in reversed(range(half_n)):
                return_copy(g, d).start()

            @pl.when(g >= my_share)
            def _():
                k = g - my_share
                ghosts = product(back[1], coeffs)
                gfil[k, 0] = ghosts[:, :128].reshape(half_n, wide, 128)
                gfil[k, 1] = ghosts[:, 128:].reshape(half_n, wide, 128)
                for d in reversed(range(half_n)):
                    ghost_copy(k, d).start()

        def step(g):
            @pl.when(g < 2 * my_share)
            def _():
                analyse(g)

            @pl.when(g == 1)
            def _():
                ready()

            @pl.when(g >= 1)
            def _():
                row = early_lo + g - 1
                sweep(row, jnp.minimum(row + 1, early_hi))
                evaluate(g - 1)

        repeat(2 * my_share + 1, step)
        sweep(early_lo + 2 * my_share, early_hi)

    @pl.when(south & hub & (hub_index == second_hub))
    def _():
        for d in range(half_n):
            second_copy(d).start()

    @pl.when(jnp.logical_not(hub))
    def _():
        ready()
        sweep(early_lo, early_hi)

    @pl.when(end)
    def _():
        def sent(g):
            for j in range(HUBS):
                @pl.when((g < 2 * SHARE[j]) & (hub_place(j) != place))
                def _():
                    forward_copy(j, g)[1].wait_send()

        repeat(2 * max(SHARE), sent)

        def take(later):
            for j in range(HUBS):

                def one(k):
                    g = later * SHARE[j] + k
                    await_bytes(caps.at[cap_slots(j, g)], rr.at[j, g])
                    c = channel(j, g)
                    slot = c * CAP + 2 * later
                    r = cap0 + cap_pair(j, g)
                    ext[c, r] = caps[slot]
                    ext[c, r + 1] = caps[slot + 1]

                repeat(SHARE[j], one)

        take(0)
        make_emfs(
            jnp.where(north, CAP - 2, rows - CAP - 1), jnp.where(north, CAP, rows - CAP + 1)
        )
        sweep(jnp.where(north, CAP - 1, rows - CAP - 2), jnp.where(north, CAP + 1, rows - CAP))
        take(1)

        for j in range(HUBS):
            for k in range(SHARE[j]):
                await_bytes(ext.at[channel(j, k), ghost_row], gr.at[j, k])

        for c in ODD:
            ext[c, ghost_row] = -ext[c, ghost_row]

        @pl.when(south)
        def _():
            await_bytes(ext.at[BTHETA, rows + 1], g2r.at[0])
            ext[BTHETA, rows + 1] = -ext[BTHETA, rows + 1]

        make_emfs(jnp.where(north, -1, rows - CAP + 1), jnp.where(north, CAP - 2, rows + 1))
        sweep(jnp.where(north, 0, rows - CAP), jnp.where(north, CAP - 1, rows))

    @pl.when(t < nt - 1)
    def _():
        down.wait_send()

    @pl.when(t > 0)
    def _():
        up.wait_send()
        up2.wait_send()

    @pl.when(hub)
    def _():
        def drain(g):
            middle_copy(g).wait_send()
            for d in range(1, half_n):
                return_copy(g, d).wait_send()

        def drain_ghost(g):
            for d in range(1, half_n):
                ghost_copy(g, d).wait_send()

        repeat(2 * my_share, drain)
        repeat(my_share, drain_ghost)

    @pl.when(south & hub & (hub_index == second_hub))
    def _():
        for d in range(1, half_n):
            second_copy(d).wait_send()


def local(n, nt, density, velocity, bfield, levels):
    _, rows, cols, radial = density.shape
    half_n = n // 2
    groups = 2 * max(SHARE)
    wide = cols + 8
    forward, back = tables(n, cols)
    any_space = pl.BlockSpec(memory_space=pl.ANY)
    vmem = pl.BlockSpec(memory_space=pltpu.VMEM)
    f32, bf16 = jnp.float32, jnp.bfloat16
    dma = pltpu.SemaphoreType.DMA
    return pl.pallas_call(
        functools.partial(kernel, n, nt, rows, cols),
        out_shape=(
            jax.ShapeDtypeStruct(density.shape, f32),
            jax.ShapeDtypeStruct(bfield.shape, f32),
        ),
        in_specs=[any_space] * 3 + [pl.BlockSpec(memory_space=pltpu.SMEM)] + [any_space] * 2,
        out_specs=(vmem, vmem),
        scratch_shapes=[
            pltpu.VMEM((CHANNELS, rows + 3, wide, radial), f32),
            pltpu.VMEM((3, rows + 2, wide, radial), f32),
            pltpu.VMEM((groups, 2, half_n * cols, radial), f32),
            pltpu.VMEM((groups, 2 * KMAX, 2 * radial), f32),
            pltpu.VMEM((groups, 2 * KMAX, 2 * radial), f32),
            pltpu.VMEM((groups, 2, half_n, wide, radial), f32),
            pltpu.VMEM((groups // 2, 2, half_n, wide, radial), f32),
            pltpu.VMEM((CHANNELS * CAP, wide, radial), f32),
            pltpu.VMEM((2, 2 * KMAX, half_n * cols), bf16),
            pltpu.VMEM((2, 2, half_n * wide, 2 * KMAX), bf16),
            pltpu.VMEM((CHANNELS, rows, radial), f32),
            pltpu.VMEM((CHANNELS + 1, rows, radial), f32),
            pltpu.VMEM((CHANNELS, rows, radial), f32),
            pltpu.VMEM((CHANNELS + 1, rows, radial), f32),
            dma((6,)),
            dma((HUBS, groups)),
            dma((groups, half_n)),
            dma((groups,)),
            dma((groups,)),
            dma((groups, half_n)),
            dma((HUBS, groups)),
            dma((groups // 2, half_n)),
            dma((HUBS, groups // 2)),
            dma((half_n,)),
            dma((1,)),
            dma((2,)),
            dma((2,)),
            dma((3,)),
            dma((3,)),
        ],
        compiler_params=pltpu.CompilerParams(
            collective_id=0, has_side_effects=True, vmem_limit_bytes=56 * 1024 * 1024
        ),
        name="substep",
    )(density, velocity, bfield, levels, jnp.asarray(forward), jnp.asarray(back))


def solution(mesh):
    spec = P(None, "theta", "phi", None)
    return jax.shard_map(
        functools.partial(local, mesh.shape["phi"], mesh.shape["theta"]),
        mesh=mesh,
        in_specs=(spec, spec, spec, P()),
        out_specs=(spec, spec),
        check_vma=False,
    )
```

```python
import functools
import math

import jax
import jax.numpy as jnp
import numpy as np
import ml_dtypes
from jax import lax
from jax.experimental import pallas as pl
from jax.experimental.pallas import tpu as pltpu
from jax.sharding import PartitionSpec as P

CAP = 4
KMAX = 128
TIME_STEP = 0.2
CHANNELS = 8
HUBS = 4
ODD = (3, 4, 6, 7)
BTHETA = 6
BPHI = 7
MESH = pl.DeviceIdType.MESH


def split_table(table):
    high = table.astype(ml_dtypes.bfloat16)
    low = (table - high.astype(np.float64)).astype(ml_dtypes.bfloat16)
    return np.stack([high, low])


def tables(count, cols):
    cycle = count * cols
    orders = np.arange(KMAX)
    points = np.arange(cycle)
    angle = (orders[:, None] * points[None, :] % cycle) * (2.0 * math.pi / cycle)
    forward = np.concatenate([np.cos(angle), np.sin(angle)], axis=0)
    offset = np.concatenate([np.arange(cols + 7), [-1]])
    place = ((np.arange(count)[:, None] * cols + offset[None, :]) % cycle).reshape(-1)
    back = forward.T[place]
    return split_table(forward), split_table(back)


def roll_left(x):
    return pltpu.roll(x, 1, 0)


def roll_right(x):
    return pltpu.roll(x, x.shape[0] - 1, 0)


def roll_below(x):
    return pltpu.roll(x, 1, 1)


def roll_above(x):
    return pltpu.roll(x, x.shape[1] - 1, 1)


def lanes(cols):
    lane = lax.broadcasted_iota(jnp.int32, (cols + 8, 128), 1)
    return lane == 0, lane == 127


def emf_row(ext, emf, j, rows, cols):
    first, last = lanes(cols)
    at = jnp.where(j < 0, rows + 2, j)
    ur, ut, up = ext[2, at], ext[3, at], ext[4, at]
    br, bt, bp = ext[5, at], ext[6, at], ext[7, at]
    bt_s = bt + ext[6, j + 1]
    br_s = br + jnp.where(last, br, roll_above(br))
    e_p = ut * br_s - ur * bt_s
    emf[0, j + 1] = e_p
    e_p0 = ut * (br + br) - ur * bt_s
    emf[1, j + 1] = e_p + jnp.where(first, e_p0, roll_below(e_p))
    e_r = up * bt_s - ut * (bp + roll_right(bp))
    emf[2, j + 1] = e_r + roll_left(e_r)


def flux_weights(hl, hr):
    most = jnp.maximum(jnp.abs(hl), jnp.abs(hr))
    return hl + most, hr - most


def stencil_row(ext, emf, dout, bout, row, rows, cols):
    first, last = lanes(cols)
    lower = jnp.where(row == 0, rows + 2, row - 1)
    upper = row + 1

    vr, vp = ext[2, row], ext[4, row]
    ht = 0.5 * ext[3, row]
    lo_l, lo_r = flux_weights(0.5 * ext[3, lower], ht)
    up_l, up_r = flux_weights(ht, 0.5 * ext[3, upper])
    middle = up_l - lo_r
    hp = 0.5 * vp
    p_l, p_r = flux_weights(roll_left(hp), hp)
    hr = 0.5 * vr
    r_l, r_r = flux_weights(jnp.where(first, hr, roll_below(hr)), hr)
    for c in range(2):
        q = ext[c, row]
        tend = middle * q + (up_r * ext[c, upper] - lo_l * ext[c, lower])
        fp = p_l * roll_left(q) + p_r * q
        fr = r_l * jnp.where(first, q, roll_below(q)) + r_r * q
        tend = tend + (roll_right(fp) - fp)
        tend = tend + (jnp.where(last, q * vr, roll_above(fr)) - fr)
        dout[c, row] = (q - TIME_STEP * tend)[:cols]

    br, bp = ext[5, row], ext[7, row]
    bp_s = bp + roll_right(bp)
    br_s = br + jnp.where(last, br, roll_above(br))
    vr_bp = vr * bp_s
    e_t = vr_bp - vp * br_s
    e_t0 = vr_bp - vp * (br + br)
    pair = e_t + roll_left(e_t)
    pair0 = e_t0 + roll_left(e_t0)
    edge_t = pair + jnp.where(first, pair0, roll_below(pair))
    scale = TIME_STEP * 0.125
    new_r = br - scale * (
        (emf[1, row + 2] - emf[1, row]) - (roll_right(edge_t) - edge_t)
    )
    bout[0, row] = new_r[:cols]
    edge_t_above = jnp.where(last, 2.0 * pair, roll_above(edge_t))
    new_p = bp - scale * ((edge_t_above - edge_t) - (emf[2, row + 2] - emf[2, row]))
    bout[2, row] = new_p[:cols]
    edge_p = emf[1, row] + emf[1, row + 1]
    edge_p_above = jnp.where(last, 2.0 * (emf[0, row] + emf[0, row + 1]), roll_above(edge_p))
    edge_r = emf[2, row] + emf[2, row + 1]
    new_t = ext[6, row] - scale * (
        (roll_right(edge_r) - edge_r) - (edge_p_above - edge_p)
    )
    bout[1, row] = new_t[:cols]


def split(x):
    high = x.astype(jnp.bfloat16)
    return high, (x - high.astype(jnp.float32)).astype(jnp.bfloat16)


def product(table, x):
    high, low = split(x)
    dot = functools.partial(jnp.dot, preferred_element_type=jnp.float32)
    return dot(table[0], high) + (dot(table[0], low) + dot(table[1], high))


def kernel(
    n, nt, rows, cols,
    density, velocity, bfield, levels, fwd_hbm, back_hbm,
    dens_hbm, field_hbm,
    ext, dout, bout, out_sem, emf, cyc, part, other_part, fil, gfil, caps, fwd, back, to_right, to_left, at_left, at_right,
    load_sem, fs, fr, ms, mr, rs, rr, gs, gr, g2s, g2r, hs, hr, ts, tr,
):
    half_n = n // 2
    groups = CHANNELS // HUBS * 2
    pole_groups = groups // 2
    wide = cols + 8
    cycle = n * cols
    t = lax.axis_index("theta")
    me = lax.axis_index("phi")
    north = t == 0
    south = t == nt - 1
    end = north | south
    cap0 = jnp.where(north, 0, rows - CAP)
    main = pl.ds(0, cols)
    half = lax.div(me, half_n)
    place = lax.rem(me, half_n)

    def hub_place(j):
        return jnp.where(half == 0, half_n - HUBS + j, j)

    hub_index = place - hub_place(0)
    hub = end & (hub_index >= 0) & (hub_index < HUBS)

    loads = [
        pltpu.make_async_copy(density, ext.at[pl.ds(0, 2), pl.ds(0, rows), main], load_sem.at[0]),
        pltpu.make_async_copy(velocity, ext.at[pl.ds(2, 3), pl.ds(0, rows), main], load_sem.at[1]),
        pltpu.make_async_copy(bfield, ext.at[pl.ds(5, 3), pl.ds(0, rows), main], load_sem.at[2]),
    ]
    width = half_n * wide
    near = pl.ds(pl.multiple_of(half * width, 16), width)
    far = pl.ds(pl.multiple_of((1 - half) * width, 16), width)
    mine = pl.ds(pl.multiple_of(half * half_n * cols, 128), half_n * cols)
    both = pl.ds(0, 2)
    modes = pl.ds(0, 2 * KMAX)
    table_loads = [
        pltpu.make_async_copy(fwd_hbm.at[both, modes, mine], fwd, load_sem.at[3]),
        pltpu.make_async_copy(back_hbm.at[both, near], back.at[0], load_sem.at[4]),
        pltpu.make_async_copy(back_hbm.at[both, far], back.at[1], load_sem.at[5]),
    ]
    for copy in loads + table_loads:
        copy.start()

    barrier = pltpu.get_barrier_semaphore()

    def other(d):
        return lax.rem(me + d, n)

    def greet(device):
        pl.semaphore_signal(barrier, inc=1, device_id=device, device_id_type=MESH)

    right, left = other(1), other(n - 1)

    @pl.when(end)
    def _():
        for d in range(1, n):
            greet({"phi": other(d)})

    @pl.when(jnp.logical_not(end))
    def _():
        greet({"phi": right})
        greet({"phi": left})

    @pl.when(t > 0)
    def _():
        greet({"theta": t - 1})

    @pl.when(t < nt - 1)
    def _():
        greet({"theta": t + 1})

    @pl.when(end)
    def _():
        pl.semaphore_wait(barrier, n)

    @pl.when(jnp.logical_not(end))
    def _():
        pl.semaphore_wait(barrier, 4)

    for copy in loads:
        copy.wait()

    def remote(src, dst, send, recv, device):
        return pltpu.make_async_remote_copy(
            src_ref=src, dst_ref=dst, send_sem=send, recv_sem=recv,
            device_id=device, device_id_type=MESH,
        )

    def await_bytes(ref, sem):
        pltpu.make_async_copy(ref, ref, sem).wait()

    def repeat(count, body):
        def step(i, carry):
            body(i)
            return carry

        lax.fori_loop(0, count, step, 0)

    def cap_pair(g):
        later = lax.div(g, pole_groups)
        return jnp.where(north, CAP - 2 - 2 * later, 2 * later)

    def channel(j, g):
        return j * pole_groups + lax.rem(g, pole_groups)

    def cap_slots(j, g):
        return pl.ds(channel(j, g) * CAP + 2 * lax.div(g, pole_groups), 2)

    def forward_copy(j, g):
        src = ext.at[channel(j, g), pl.ds(cap0 + cap_pair(g), 2), main]
        dst = cyc.at[g, both, pl.ds(pl.multiple_of(place * cols, 8), cols)]
        device = half * half_n + hub_place(j)
        return (
            pltpu.make_async_copy(src, dst, fr.at[g, place]),
            remote(src, dst, fs.at[j, g], fr.at[g, place], {"phi": device}),
        )

    def middle_copy(g):
        partner = jnp.where(half == 0, half_n, half_n - HUBS) + hub_index
        return remote(part.at[g], other_part.at[g], ms.at[g], mr.at[g], {"phi": partner})

    def target(d):
        spot = lax.rem(place + d, half_n)
        return spot, half * half_n + spot

    def return_copy(g, d):
        spot, device = target(d)
        src = fil.at[g, both, spot]
        dst = caps.at[cap_slots(hub_index, g)]
        sem = rr.at[hub_index, g]
        if d == 0:
            return pltpu.make_async_copy(src, dst, sem)
        return remote(src, dst, rs.at[g, d], sem, {"phi": device})

    ghost_row = jnp.where(north, rows + 2, rows)

    def ghost_copy(g, d):
        spot, device = target(d)
        src = gfil.at[g, jnp.where(north, 0, 1), spot]
        dst = ext.at[channel(hub_index, g), ghost_row]
        sem = gr.at[hub_index, g]
        if d == 0:
            return pltpu.make_async_copy(src, dst, sem)
        return remote(src, dst, gs.at[g, d], sem, {"phi": device})

    second_hub, second_group = BTHETA // pole_groups, BTHETA % pole_groups

    def second_copy(d):
        spot, device = target(d)
        src = gfil.at[second_group, 0, spot]
        dst = ext.at[BTHETA, rows + 1]
        if d == 0:
            return pltpu.make_async_copy(src, dst, g2r.at[0])
        return remote(src, dst, g2s.at[d], g2r.at[0], {"phi": device})

    for c in range(CHANNELS):
        to_right[c] = ext[c, 0:rows, cols - 1]
        to_left[c] = ext[c, 0:rows, 0]
    to_left[CHANNELS] = ext[BPHI, 0:rows, 1]

    go_right = remote(to_right, at_left, hs.at[0], hr.at[0], {"phi": right})
    go_left = remote(to_left, at_right, hs.at[1], hr.at[1], {"phi": left})
    go_right.start()
    go_left.start()

    @pl.when(end)
    def _():
        def send(g):
            for j in range(HUBS):
                here, away = forward_copy(j, g)

                @pl.when(hub_place(j) == place)
                def _():
                    here.start()

                @pl.when(hub_place(j) != place)
                def _():
                    away.start()

        repeat(groups, send)

    go_right.wait()
    go_left.wait()

    def unpack(lo, hi):
        for c in range(CHANNELS):
            ext[c, lo:hi, wide - 1] = at_left[c, lo:hi]
            ext[c, lo:hi, cols] = at_right[c, lo:hi]
        ext[BPHI, lo:hi, cols + 1] = at_right[CHANNELS, lo:hi]

    @pl.when(north)
    def _():
        unpack(CAP, rows)

    @pl.when(south)
    def _():
        unpack(0, rows - CAP)

    @pl.when(jnp.logical_not(end))
    def _():
        unpack(0, rows)

    every = pl.ds(0, CHANNELS)
    down = remote(ext.at[every, rows - 1], ext.at[every, rows + 2], ts.at[0], tr.at[0], {"theta": t + 1})
    up = remote(ext.at[every, 0], ext.at[every, rows], ts.at[1], tr.at[1], {"theta": t - 1})
    up2 = remote(ext.at[BTHETA, 1], ext.at[BTHETA, rows + 1], ts.at[2], tr.at[2], {"theta": t - 1})

    @pl.when(t < nt - 1)
    def _():
        down.start()

    @pl.when(t > 0)
    def _():
        up.start()
        up2.start()

    for copy in table_loads:
        copy.wait()

    def row_copies(row):
        return (
            pltpu.make_async_copy(dout.at[pl.ds(0, 2), row], dens_hbm.at[pl.ds(0, 2), row], out_sem.at[0, row]),
            pltpu.make_async_copy(bout.at[pl.ds(0, 3), row], field_hbm.at[pl.ds(0, 3), row], out_sem.at[1, row]),
        )

    def sweep(lo, hi):
        def body(row, carry):
            stencil_row(ext, emf, dout, bout, row, rows, cols)
            for copy in row_copies(row):
                copy.start()
            return carry

        lax.fori_loop(lo, hi, body, 0)

    def make_emfs(lo, hi):
        def body(j, carry):
            emf_row(ext, emf, j, rows, cols)
            return carry

        lax.fori_loop(lo, hi, body, 0)

    early_lo = jnp.where(north, CAP + 1, 0)
    early_hi = jnp.where(south, rows - CAP - 2, rows)

    def ready():
        @pl.when(t > 0)
        def _():
            down.wait_recv()

        @pl.when(t < nt - 1)
        def _():
            up.wait_recv()
            up2.wait_recv()

        make_emfs(jnp.where(north, CAP, -1), jnp.where(south, rows - CAP - 1, rows + 1))

    @pl.when(hub)
    def _():
        pole = jnp.where(north, 0, 1)
        mode = lax.rem(lax.broadcasted_iota(jnp.int32, (2 * KMAX, 128), 0), KMAX)
        weight = jnp.where(mode == 0, 1.0 / cycle, 2.0 / cycle)

        def analyse(g):
            for i in range(half_n):
                await_bytes(cyc.at[g, both, pl.ds(i * cols, cols)], fr.at[g, i])
            part[g] = product(fwd, jnp.concatenate([cyc[g, 0], cyc[g, 1]], axis=1))
            middle_copy(g).start()

        def evaluate(g):
            await_bytes(other_part.at[g], mr.at[g])
            masks = []
            for s in range(2):
                limit = lax.shift_right_logical(jnp.int32(KMAX), levels[pole, cap_pair(g) + s])
                masks.append(jnp.where(mode < limit, weight, 0.0))
            coeffs = (part[g] + other_part[g]) * jnp.concatenate(masks, axis=1)
            values = product(back[0], coeffs)
            fil[g, 0] = values[:, :128].reshape(half_n, wide, 128)
            fil[g, 1] = values[:, 128:].reshape(half_n, wide, 128)
            for d in reversed(range(half_n)):
                return_copy(g, d).start()

            @pl.when(g >= pole_groups)
            def _():
                k = g - pole_groups
                ghosts = product(back[1], coeffs)
                gfil[k, 0] = ghosts[:, :128].reshape(half_n, wide, 128)
                gfil[k, 1] = ghosts[:, 128:].reshape(half_n, wide, 128)
                for d in reversed(range(half_n)):
                    ghost_copy(k, d).start()

        repeat(groups, analyse)
        ready()

        def step(g):
            row = early_lo + g
            sweep(row, jnp.minimum(row + 1, early_hi))
            evaluate(g)

        repeat(groups, step)
        sweep(early_lo + groups, early_hi)

    @pl.when(south & hub & (hub_index == second_hub))
    def _():
        for d in range(half_n):
            second_copy(d).start()

    @pl.when(jnp.logical_not(hub))
    def _():
        ready()
        sweep(early_lo, early_hi)

    @pl.when(end)
    def _():
        def sent(g):
            for j in range(HUBS):
                @pl.when(hub_place(j) != place)
                def _():
                    forward_copy(j, g)[1].wait_send()

        repeat(groups, sent)

        def take(first):
            def one(k):
                g = first + k
                for j in range(HUBS):
                    slots = cap_slots(j, g)
                    await_bytes(caps.at[slots], rr.at[j, g])
                    c = channel(j, g)
                    slot = c * CAP + 2 * lax.div(g, pole_groups)
                    r = cap0 + cap_pair(g)
                    ext[c, r] = caps[slot]
                    ext[c, r + 1] = caps[slot + 1]

            repeat(pole_groups, one)

        take(0)
        make_emfs(
            jnp.where(north, CAP - 2, rows - CAP - 1), jnp.where(north, CAP, rows - CAP + 1)
        )
        sweep(jnp.where(north, CAP - 1, rows - CAP - 2), jnp.where(north, CAP + 1, rows - CAP))
        take(pole_groups)

        def ghost(k):
            for j in range(HUBS):
                await_bytes(ext.at[channel(j, k), ghost_row], gr.at[j, k])

        repeat(pole_groups, ghost)
        for c in ODD:
            ext[c, ghost_row] = -ext[c, ghost_row]

        @pl.when(south)
        def _():
            await_bytes(ext.at[BTHETA, rows + 1], g2r.at[0])
            ext[BTHETA, rows + 1] = -ext[BTHETA, rows + 1]

        make_emfs(jnp.where(north, -1, rows - CAP + 1), jnp.where(north, CAP - 2, rows + 1))
        sweep(jnp.where(north, 0, rows - CAP), jnp.where(north, CAP - 1, rows))

    def wait_row(row):
        for copy in row_copies(row):
            copy.wait()

    repeat(rows, wait_row)

    @pl.when(t < nt - 1)
    def _():
        down.wait_send()

    @pl.when(t > 0)
    def _():
        up.wait_send()
        up2.wait_send()

    @pl.when(hub)
    def _():
        def drain(g):
            middle_copy(g).wait_send()
            for d in range(1, half_n):
                return_copy(g, d).wait_send()

        def drain_ghost(g):
            for d in range(1, half_n):
                ghost_copy(g, d).wait_send()

        repeat(groups, drain)
        repeat(pole_groups, drain_ghost)

    @pl.when(south & hub & (hub_index == second_hub))
    def _():
        for d in range(1, half_n):
            second_copy(d).wait_send()


def local(n, nt, density, velocity, bfield, levels):
    _, rows, cols, radial = density.shape
    half_n = n // 2
    groups = CHANNELS // HUBS * 2
    wide = cols + 8
    forward, back = tables(n, cols)
    any_space = pl.BlockSpec(memory_space=pl.ANY)
    f32, bf16 = jnp.float32, jnp.bfloat16
    dma = pltpu.SemaphoreType.DMA
    return pl.pallas_call(
        functools.partial(kernel, n, nt, rows, cols),
        out_shape=(
            jax.ShapeDtypeStruct(density.shape, f32),
            jax.ShapeDtypeStruct(bfield.shape, f32),
        ),
        in_specs=[any_space] * 3 + [pl.BlockSpec(memory_space=pltpu.SMEM)] + [any_space] * 2,
        out_specs=(any_space, any_space),
        scratch_shapes=[
            pltpu.VMEM((CHANNELS, rows + 3, wide, radial), f32),
            pltpu.VMEM(density.shape, f32),
            pltpu.VMEM(bfield.shape, f32),
            dma((2, rows)),
            pltpu.VMEM((3, rows + 2, wide, radial), f32),
            pltpu.VMEM((groups, 2, half_n * cols, radial), f32),
            pltpu.VMEM((groups, 2 * KMAX, 2 * radial), f32),
            pltpu.VMEM((groups, 2 * KMAX, 2 * radial), f32),
            pltpu.VMEM((groups, 2, half_n, wide, radial), f32),
            pltpu.VMEM((groups // 2, 2, half_n, wide, radial), f32),
            pltpu.VMEM((CHANNELS * CAP, wide, radial), f32),
            pltpu.VMEM((2, 2 * KMAX, half_n * cols), bf16),
            pltpu.VMEM((2, 2, half_n * wide, 2 * KMAX), bf16),
            pltpu.VMEM((CHANNELS, rows, radial), f32),
            pltpu.VMEM((CHANNELS + 1, rows, radial), f32),
            pltpu.VMEM((CHANNELS, rows, radial), f32),
            pltpu.VMEM((CHANNELS + 1, rows, radial), f32),
            dma((6,)),
            dma((HUBS, groups)),
            dma((groups, half_n)),
            dma((groups,)),
            dma((groups,)),
            dma((groups, half_n)),
            dma((HUBS, groups)),
            dma((groups // 2, half_n)),
            dma((HUBS, groups // 2)),
            dma((half_n,)),
            dma((1,)),
            dma((2,)),
            dma((2,)),
            dma((3,)),
            dma((3,)),
        ],
        compiler_params=pltpu.CompilerParams(
            collective_id=0, has_side_effects=True, vmem_limit_bytes=56 * 1024 * 1024
        ),
        name="substep",
    )(density, velocity, bfield, levels, jnp.asarray(forward), jnp.asarray(back))


def solution(mesh):
    spec = P(None, "theta", "phi", None)
    return jax.shard_map(
        functools.partial(local, mesh.shape["phi"], mesh.shape["theta"]),
        mesh=mesh,
        in_specs=(spec, spec, spec, P()),
        out_specs=(spec, spec),
        check_vma=False,
    )
```

```python
import functools
import math

import jax
import jax.numpy as jnp
import numpy as np
import ml_dtypes
from jax import lax
from jax.experimental import pallas as pl
from jax.experimental.pallas import tpu as pltpu
from jax.sharding import PartitionSpec as P

CAP = 4
KMAX = 128
TIME_STEP = 0.2
CHANNELS = 8
HUBS = 4
ODD = (3, 4, 6, 7)
BTHETA = 6
BPHI = 7
MESH = pl.DeviceIdType.MESH


def split_table(table):
    high = table.astype(ml_dtypes.bfloat16)
    low = (table - high.astype(np.float64)).astype(ml_dtypes.bfloat16)
    return np.stack([high, low])


def tables(count, cols):
    cycle = count * cols
    orders = np.arange(KMAX)
    points = np.arange(cycle)
    angle = (orders[:, None] * points[None, :] % cycle) * (2.0 * math.pi / cycle)
    forward = np.concatenate([np.cos(angle), np.sin(angle)], axis=0)
    offset = np.concatenate([np.arange(cols + 7), [-1]])
    place = ((np.arange(count)[:, None] * cols + offset[None, :]) % cycle).reshape(-1)
    back = forward.T[place]
    return split_table(forward), split_table(back)


def roll_left(x):
    return pltpu.roll(x, 1, 0)


def roll_right(x):
    return pltpu.roll(x, x.shape[0] - 1, 0)


def roll_below(x):
    return pltpu.roll(x, 1, 1)


def roll_above(x):
    return pltpu.roll(x, x.shape[1] - 1, 1)


def lanes(cols):
    lane = lax.broadcasted_iota(jnp.int32, (cols + 8, 128), 1)
    return lane == 0, lane == 127


def emf_row(ext, emf, j, rows, cols):
    first, last = lanes(cols)
    at = jnp.where(j < 0, rows + 2, j)
    ur, ut, up = ext[2, at], ext[3, at], ext[4, at]
    br, bt, bp = ext[5, at], ext[6, at], ext[7, at]
    bt_s = bt + ext[6, j + 1]
    br_s = br + jnp.where(last, br, roll_above(br))
    e_p = ut * br_s - ur * bt_s
    emf[0, j + 1] = e_p
    e_p0 = ut * (br + br) - ur * bt_s
    emf[1, j + 1] = e_p + jnp.where(first, e_p0, roll_below(e_p))
    e_r = up * bt_s - ut * (bp + roll_right(bp))
    emf[2, j + 1] = e_r + roll_left(e_r)


def flux_weights(hl, hr):
    most = jnp.maximum(jnp.abs(hl), jnp.abs(hr))
    return hl + most, hr - most


def stencil_row(ext, emf, dout, bout, row, rows, cols):
    first, last = lanes(cols)
    lower = jnp.where(row == 0, rows + 2, row - 1)
    upper = row + 1

    vr, vp = ext[2, row], ext[4, row]
    ht = 0.5 * ext[3, row]
    lo_l, lo_r = flux_weights(0.5 * ext[3, lower], ht)
    up_l, up_r = flux_weights(ht, 0.5 * ext[3, upper])
    middle = up_l - lo_r
    hp = 0.5 * vp
    p_l, p_r = flux_weights(roll_left(hp), hp)
    hr = 0.5 * vr
    r_l, r_r = flux_weights(jnp.where(first, hr, roll_below(hr)), hr)
    for c in range(2):
        q = ext[c, row]
        tend = middle * q + (up_r * ext[c, upper] - lo_l * ext[c, lower])
        fp = p_l * roll_left(q) + p_r * q
        fr = r_l * jnp.where(first, q, roll_below(q)) + r_r * q
        tend = tend + (roll_right(fp) - fp)
        tend = tend + (jnp.where(last, q * vr, roll_above(fr)) - fr)
        dout[c, row] = (q - TIME_STEP * tend)[:cols]

    br, bp = ext[5, row], ext[7, row]
    bp_s = bp + roll_right(bp)
    br_s = br + jnp.where(last, br, roll_above(br))
    vr_bp = vr * bp_s
    e_t = vr_bp - vp * br_s
    e_t0 = vr_bp - vp * (br + br)
    pair = e_t + roll_left(e_t)
    pair0 = e_t0 + roll_left(e_t0)
    edge_t = pair + jnp.where(first, pair0, roll_below(pair))
    scale = TIME_STEP * 0.125
    new_r = br - scale * (
        (emf[1, row + 2] - emf[1, row]) - (roll_right(edge_t) - edge_t)
    )
    bout[0, row] = new_r[:cols]
    edge_t_above = jnp.where(last, 2.0 * pair, roll_above(edge_t))
    new_p = bp - scale * ((edge_t_above - edge_t) - (emf[2, row + 2] - emf[2, row]))
    bout[2, row] = new_p[:cols]
    edge_p = emf[1, row] + emf[1, row + 1]
    edge_p_above = jnp.where(last, 2.0 * (emf[0, row] + emf[0, row + 1]), roll_above(edge_p))
    edge_r = emf[2, row] + emf[2, row + 1]
    new_t = ext[6, row] - scale * (
        (roll_right(edge_r) - edge_r) - (edge_p_above - edge_p)
    )
    bout[1, row] = new_t[:cols]


def split(x):
    high = x.astype(jnp.bfloat16)
    return high, (x - high.astype(jnp.float32)).astype(jnp.bfloat16)


def product(table, x):
    high, low = split(x)
    dot = functools.partial(jnp.dot, preferred_element_type=jnp.float32)
    return dot(table[0], high) + (dot(table[0], low) + dot(table[1], high))


def kernel(
    n, nt, rows, cols,
    density, velocity, bfield, levels, fwd_hbm, back_hbm,
    dens_hbm, field_hbm,
    ext, dout, bout, out_sem, emf, cyc, part, other_part, fil, gfil, caps, fwd, back, to_right, to_left, at_left, at_right,
    load_sem, fs, fr, ms, mr, rs, rr, gs, gr, g2s, g2r, hs, hr, ts, tr,
):
    half_n = n // 2
    groups = CHANNELS // HUBS * 2
    pole_groups = groups // 2
    wide = cols + 8
    cycle = n * cols
    t = lax.axis_index("theta")
    me = lax.axis_index("phi")
    north = t == 0
    south = t == nt - 1
    end = north | south
    cap0 = jnp.where(north, 0, rows - CAP)
    main = pl.ds(0, cols)
    half = lax.div(me, half_n)
    place = lax.rem(me, half_n)

    def hub_place(j):
        return jnp.where(half == 0, half_n - HUBS + j, j)

    hub_index = place - hub_place(0)
    hub = end & (hub_index >= 0) & (hub_index < HUBS)

    loads = [
        pltpu.make_async_copy(density, ext.at[pl.ds(0, 2), pl.ds(0, rows), main], load_sem.at[0]),
        pltpu.make_async_copy(velocity, ext.at[pl.ds(2, 3), pl.ds(0, rows), main], load_sem.at[1]),
        pltpu.make_async_copy(bfield, ext.at[pl.ds(5, 3), pl.ds(0, rows), main], load_sem.at[2]),
    ]
    width = half_n * wide
    near = pl.ds(pl.multiple_of(half * width, 16), width)
    far = pl.ds(pl.multiple_of((1 - half) * width, 16), width)
    mine = pl.ds(pl.multiple_of(half * half_n * cols, 128), half_n * cols)
    both = pl.ds(0, 2)
    modes = pl.ds(0, 2 * KMAX)
    table_loads = [
        pltpu.make_async_copy(fwd_hbm.at[both, modes, mine], fwd, load_sem.at[3]),
        pltpu.make_async_copy(back_hbm.at[both, near], back.at[0], load_sem.at[4]),
        pltpu.make_async_copy(back_hbm.at[both, far], back.at[1], load_sem.at[5]),
    ]
    barrier = pltpu.get_barrier_semaphore()

    def other(d):
        return lax.rem(me + d, n)

    def greet(device):
        pl.semaphore_signal(barrier, inc=1, device_id=device, device_id_type=MESH)

    right, left = other(1), other(n - 1)

    @pl.when(end)
    def _():
        for d in range(1, n):
            greet({"phi": other(d)})

    @pl.when(jnp.logical_not(end))
    def _():
        greet({"phi": right})
        greet({"phi": left})

    @pl.when(t > 0)
    def _():
        greet({"theta": t - 1})

    @pl.when(t < nt - 1)
    def _():
        greet({"theta": t + 1})

    for copy in loads + table_loads:
        copy.start()

    @pl.when(end)
    def _():
        pl.semaphore_wait(barrier, n)

    @pl.when(jnp.logical_not(end))
    def _():
        pl.semaphore_wait(barrier, 4)

    for copy in loads:
        copy.wait()

    def remote(src, dst, send, recv, device):
        return pltpu.make_async_remote_copy(
            src_ref=src, dst_ref=dst, send_sem=send, recv_sem=recv,
            device_id=device, device_id_type=MESH,
        )

    def await_bytes(ref, sem):
        pltpu.make_async_copy(ref, ref, sem).wait()

    def repeat(count, body):
        def step(i, carry):
            body(i)
            return carry

        lax.fori_loop(0, count, step, 0)

    def cap_pair(g):
        later = lax.div(g, pole_groups)
        return jnp.where(north, CAP - 2 - 2 * later, 2 * later)

    def channel(j, g):
        return j * pole_groups + lax.rem(g, pole_groups)

    def cap_slots(j, g):
        return pl.ds(channel(j, g) * CAP + 2 * lax.div(g, pole_groups), 2)

    def forward_copy(j, g):
        src = ext.at[channel(j, g), pl.ds(cap0 + cap_pair(g), 2), main]
        dst = cyc.at[g, both, pl.ds(pl.multiple_of(place * cols, 8), cols)]
        device = half * half_n + hub_place(j)
        return (
            pltpu.make_async_copy(src, dst, fr.at[g, place]),
            remote(src, dst, fs.at[j, g], fr.at[g, place], {"phi": device}),
        )

    def middle_copy(g):
        partner = jnp.where(half == 0, half_n, half_n - HUBS) + hub_index
        return remote(part.at[g], other_part.at[g], ms.at[g], mr.at[g], {"phi": partner})

    def target(d):
        spot = lax.rem(place + d, half_n)
        return spot, half * half_n + spot

    def return_copy(g, d):
        spot, device = target(d)
        src = fil.at[g, both, spot]
        dst = caps.at[cap_slots(hub_index, g)]
        sem = rr.at[hub_index, g]
        if d == 0:
            return pltpu.make_async_copy(src, dst, sem)
        return remote(src, dst, rs.at[g, d], sem, {"phi": device})

    ghost_row = jnp.where(north, rows + 2, rows)

    def ghost_copy(g, d):
        spot, device = target(d)
        src = gfil.at[g, jnp.where(north, 0, 1), spot]
        dst = ext.at[channel(hub_index, g), ghost_row]
        sem = gr.at[hub_index, g]
        if d == 0:
            return pltpu.make_async_copy(src, dst, sem)
        return remote(src, dst, gs.at[g, d], sem, {"phi": device})

    second_hub, second_group = BTHETA // pole_groups, BTHETA % pole_groups

    def second_copy(d):
        spot, device = target(d)
        src = gfil.at[second_group, 0, spot]
        dst = ext.at[BTHETA, rows + 1]
        if d == 0:
            return pltpu.make_async_copy(src, dst, g2r.at[0])
        return remote(src, dst, g2s.at[d], g2r.at[0], {"phi": device})

    for c in range(CHANNELS):
        to_right[c] = ext[c, 0:rows, cols - 1]
        to_left[c] = ext[c, 0:rows, 0]
    to_left[CHANNELS] = ext[BPHI, 0:rows, 1]

    go_right = remote(to_right, at_left, hs.at[0], hr.at[0], {"phi": right})
    go_left = remote(to_left, at_right, hs.at[1], hr.at[1], {"phi": left})
    go_right.start()
    go_left.start()

    @pl.when(end)
    def _():
        def send(g):
            for j in range(HUBS):
                here, away = forward_copy(j, g)

                @pl.when(hub_place(j) == place)
                def _():
                    here.start()

                @pl.when(hub_place(j) != place)
                def _():
                    away.start()

        repeat(groups, send)

    for copy in table_loads:
        copy.wait()

    @pl.when(hub)
    def _():
        def analyse(g):
            for i in range(half_n):
                await_bytes(cyc.at[g, both, pl.ds(i * cols, cols)], fr.at[g, i])
            part[g] = product(fwd, jnp.concatenate([cyc[g, 0], cyc[g, 1]], axis=1))
            middle_copy(g).start()

        repeat(groups, analyse)

    go_right.wait()
    go_left.wait()

    def unpack(lo, hi):
        for c in range(CHANNELS):
            ext[c, lo:hi, wide - 1] = at_left[c, lo:hi]
            ext[c, lo:hi, cols] = at_right[c, lo:hi]
        ext[BPHI, lo:hi, cols + 1] = at_right[CHANNELS, lo:hi]

    @pl.when(north)
    def _():
        unpack(CAP, rows)

    @pl.when(south)
    def _():
        unpack(0, rows - CAP)

    @pl.when(jnp.logical_not(end))
    def _():
        unpack(0, rows)

    every = pl.ds(0, CHANNELS)
    down = remote(ext.at[every, rows - 1], ext.at[every, rows + 2], ts.at[0], tr.at[0], {"theta": t + 1})
    up = remote(ext.at[every, 0], ext.at[every, rows], ts.at[1], tr.at[1], {"theta": t - 1})
    up2 = remote(ext.at[BTHETA, 1], ext.at[BTHETA, rows + 1], ts.at[2], tr.at[2], {"theta": t - 1})

    @pl.when(t < nt - 1)
    def _():
        down.start()

    @pl.when(t > 0)
    def _():
        up.start()
        up2.start()

    def row_copies(row):
        return (
            pltpu.make_async_copy(dout.at[pl.ds(0, 2), row], dens_hbm.at[pl.ds(0, 2), row], out_sem.at[0, row]),
            pltpu.make_async_copy(bout.at[pl.ds(0, 3), row], field_hbm.at[pl.ds(0, 3), row], out_sem.at[1, row]),
        )

    def sweep(lo, hi):
        def body(row, carry):
            stencil_row(ext, emf, dout, bout, row, rows, cols)
            for copy in row_copies(row):
                copy.start()
            return carry

        lax.fori_loop(lo, hi, body, 0)

    def make_emfs(lo, hi):
        def body(j, carry):
            emf_row(ext, emf, j, rows, cols)
            return carry

        lax.fori_loop(lo, hi, body, 0)

    early_lo = jnp.where(north, CAP + 1, 0)
    early_hi = jnp.where(south, rows - CAP - 2, rows)

    def ready():
        @pl.when(t > 0)
        def _():
            down.wait_recv()

        @pl.when(t < nt - 1)
        def _():
            up.wait_recv()
            up2.wait_recv()

        make_emfs(jnp.where(north, CAP, -1), jnp.where(south, rows - CAP - 1, rows + 1))

    @pl.when(hub)
    def _():
        pole = jnp.where(north, 0, 1)
        mode = lax.rem(lax.broadcasted_iota(jnp.int32, (2 * KMAX, 128), 0), KMAX)
        weight = jnp.where(mode == 0, 1.0 / cycle, 2.0 / cycle)

        def evaluate(g):
            await_bytes(other_part.at[g], mr.at[g])
            masks = []
            for s in range(2):
                limit = lax.shift_right_logical(jnp.int32(KMAX), levels[pole, cap_pair(g) + s])
                masks.append(jnp.where(mode < limit, weight, 0.0))
            coeffs = (part[g] + other_part[g]) * jnp.concatenate(masks, axis=1)
            values = product(back[0], coeffs)
            fil[g, 0] = values[:, :128].reshape(half_n, wide, 128)
            fil[g, 1] = values[:, 128:].reshape(half_n, wide, 128)
            for d in reversed(range(half_n)):
                return_copy(g, d).start()

            @pl.when(g >= pole_groups)
            def _():
                k = g - pole_groups
                ghosts = product(back[1], coeffs)
                gfil[k, 0] = ghosts[:, :128].reshape(half_n, wide, 128)
                gfil[k, 1] = ghosts[:, 128:].reshape(half_n, wide, 128)
                for d in reversed(range(half_n)):
                    ghost_copy(k, d).start()

        ready()

        def step(g):
            row = early_lo + g
            sweep(row, jnp.minimum(row + 1, early_hi))
            evaluate(g)

        repeat(groups, step)
        sweep(early_lo + groups, early_hi)

    @pl.when(south & hub & (hub_index == second_hub))
    def _():
        for d in range(half_n):
            second_copy(d).start()

    @pl.when(jnp.logical_not(hub))
    def _():
        ready()
        sweep(early_lo, early_hi)

    @pl.when(end)
    def _():
        def sent(g):
            for j in range(HUBS):
                @pl.when(hub_place(j) != place)
                def _():
                    forward_copy(j, g)[1].wait_send()

        repeat(groups, sent)

        def take(first):
            def one(k):
                g = first + k
                for j in range(HUBS):
                    slots = cap_slots(j, g)
                    await_bytes(caps.at[slots], rr.at[j, g])
                    c = channel(j, g)
                    slot = c * CAP + 2 * lax.div(g, pole_groups)
                    r = cap0 + cap_pair(g)
                    ext[c, r] = caps[slot]
                    ext[c, r + 1] = caps[slot + 1]

            repeat(pole_groups, one)

        take(0)
        make_emfs(
            jnp.where(north, CAP - 2, rows - CAP - 1), jnp.where(north, CAP, rows - CAP + 1)
        )
        sweep(jnp.where(north, CAP - 1, rows - CAP - 2), jnp.where(north, CAP + 1, rows - CAP))
        take(pole_groups)

        def ghost(k):
            for j in range(HUBS):
                await_bytes(ext.at[channel(j, k), ghost_row], gr.at[j, k])

        repeat(pole_groups, ghost)
        for c in ODD:
            ext[c, ghost_row] = -ext[c, ghost_row]

        @pl.when(south)
        def _():
            await_bytes(ext.at[BTHETA, rows + 1], g2r.at[0])
            ext[BTHETA, rows + 1] = -ext[BTHETA, rows + 1]

        make_emfs(jnp.where(north, -1, rows - CAP + 1), jnp.where(north, CAP - 2, rows + 1))
        sweep(jnp.where(north, 0, rows - CAP), jnp.where(north, CAP - 1, rows))

    def wait_row(row):
        for copy in row_copies(row):
            copy.wait()

    repeat(rows, wait_row)

    @pl.when(t < nt - 1)
    def _():
        down.wait_send()

    @pl.when(t > 0)
    def _():
        up.wait_send()
        up2.wait_send()

    @pl.when(hub)
    def _():
        def drain(g):
            middle_copy(g).wait_send()
            for d in range(1, half_n):
                return_copy(g, d).wait_send()

        def drain_ghost(g):
            for d in range(1, half_n):
                ghost_copy(g, d).wait_send()

        repeat(groups, drain)
        repeat(pole_groups, drain_ghost)

    @pl.when(south & hub & (hub_index == second_hub))
    def _():
        for d in range(1, half_n):
            second_copy(d).wait_send()


def local(n, nt, density, velocity, bfield, levels):
    _, rows, cols, radial = density.shape
    half_n = n // 2
    groups = CHANNELS // HUBS * 2
    wide = cols + 8
    forward, back = tables(n, cols)
    any_space = pl.BlockSpec(memory_space=pl.ANY)
    f32, bf16 = jnp.float32, jnp.bfloat16
    dma = pltpu.SemaphoreType.DMA
    return pl.pallas_call(
        functools.partial(kernel, n, nt, rows, cols),
        out_shape=(
            jax.ShapeDtypeStruct(density.shape, f32),
            jax.ShapeDtypeStruct(bfield.shape, f32),
        ),
        in_specs=[any_space] * 3 + [pl.BlockSpec(memory_space=pltpu.SMEM)] + [any_space] * 2,
        out_specs=(any_space, any_space),
        scratch_shapes=[
            pltpu.VMEM((CHANNELS, rows + 3, wide, radial), f32),
            pltpu.VMEM(density.shape, f32),
            pltpu.VMEM(bfield.shape, f32),
            dma((2, rows)),
            pltpu.VMEM((3, rows + 2, wide, radial), f32),
            pltpu.VMEM((groups, 2, half_n * cols, radial), f32),
            pltpu.VMEM((groups, 2 * KMAX, 2 * radial), f32),
            pltpu.VMEM((groups, 2 * KMAX, 2 * radial), f32),
            pltpu.VMEM((groups, 2, half_n, wide, radial), f32),
            pltpu.VMEM((groups // 2, 2, half_n, wide, radial), f32),
            pltpu.VMEM((CHANNELS * CAP, wide, radial), f32),
            pltpu.VMEM((2, 2 * KMAX, half_n * cols), bf16),
            pltpu.VMEM((2, 2, half_n * wide, 2 * KMAX), bf16),
            pltpu.VMEM((CHANNELS, rows, radial), f32),
            pltpu.VMEM((CHANNELS + 1, rows, radial), f32),
            pltpu.VMEM((CHANNELS, rows, radial), f32),
            pltpu.VMEM((CHANNELS + 1, rows, radial), f32),
            dma((6,)),
            dma((HUBS, groups)),
            dma((groups, half_n)),
            dma((groups,)),
            dma((groups,)),
            dma((groups, half_n)),
            dma((HUBS, groups)),
            dma((groups // 2, half_n)),
            dma((HUBS, groups // 2)),
            dma((half_n,)),
            dma((1,)),
            dma((2,)),
            dma((2,)),
            dma((3,)),
            dma((3,)),
        ],
        compiler_params=pltpu.CompilerParams(
            collective_id=0, has_side_effects=True, vmem_limit_bytes=56 * 1024 * 1024
        ),
        name="substep",
    )(density, velocity, bfield, levels, jnp.asarray(forward), jnp.asarray(back))


def solution(mesh):
    spec = P(None, "theta", "phi", None)
    return jax.shard_map(
        functools.partial(local, mesh.shape["phi"], mesh.shape["theta"]),
        mesh=mesh,
        in_specs=(spec, spec, spec, P()),
        out_specs=(spec, spec),
        check_vma=False,
    )
```

```python
import functools
import math

import jax
import jax.numpy as jnp
import numpy as np
import ml_dtypes
from jax import lax
from jax.experimental import pallas as pl
from jax.experimental.pallas import tpu as pltpu
from jax.sharding import PartitionSpec as P

CAP = 4
KMAX = 128
TIME_STEP = 0.2
CHANNELS = 8
HUBS = 4
ODD = (3, 4, 6, 7)
BTHETA = 6
BPHI = 7
MESH = pl.DeviceIdType.MESH


def split_table(table):
    high = table.astype(ml_dtypes.bfloat16)
    low = (table - high.astype(np.float64)).astype(ml_dtypes.bfloat16)
    return np.stack([high, low])


def tables(count, cols):
    cycle = count * cols
    orders = np.arange(KMAX)
    points = np.arange(cycle)
    angle = (orders[:, None] * points[None, :] % cycle) * (2.0 * math.pi / cycle)
    forward = np.concatenate([np.cos(angle), np.sin(angle)], axis=0)
    offset = np.concatenate([np.arange(cols + 7), [-1]])
    place = ((np.arange(count)[:, None] * cols + offset[None, :]) % cycle).reshape(-1)
    back = forward.T[place]
    return split_table(forward), split_table(back)


def roll_left(x):
    return pltpu.roll(x, 1, 0)


def roll_right(x):
    return pltpu.roll(x, x.shape[0] - 1, 0)


def roll_below(x):
    return pltpu.roll(x, 1, 1)


def roll_above(x):
    return pltpu.roll(x, x.shape[1] - 1, 1)


def lanes(cols):
    lane = lax.broadcasted_iota(jnp.int32, (cols + 8, 128), 1)
    return lane == 0, lane == 127


def emf_row(ext, emf, j, rows, cols):
    first, last = lanes(cols)
    at = jnp.where(j < 0, rows + 2, j)
    ur, ut, up = ext[2, at], ext[3, at], ext[4, at]
    br, bt, bp = ext[5, at], ext[6, at], ext[7, at]
    bt_s = bt + ext[6, j + 1]
    br_s = br + jnp.where(last, br, roll_above(br))
    e_p = ut * br_s - ur * bt_s
    emf[0, j + 1] = e_p
    e_p0 = ut * (br + br) - ur * bt_s
    emf[1, j + 1] = e_p + jnp.where(first, e_p0, roll_below(e_p))
    e_r = up * bt_s - ut * (bp + roll_right(bp))
    emf[2, j + 1] = e_r + roll_left(e_r)


def flux_weights(hl, hr):
    most = jnp.maximum(jnp.abs(hl), jnp.abs(hr))
    return hl + most, hr - most


def stencil_row(ext, emf, dout, bout, row, rows, cols):
    first, last = lanes(cols)
    lower = jnp.where(row == 0, rows + 2, row - 1)
    upper = row + 1

    vr, vp = ext[2, row], ext[4, row]
    ht = 0.5 * ext[3, row]
    lo_l, lo_r = flux_weights(0.5 * ext[3, lower], ht)
    up_l, up_r = flux_weights(ht, 0.5 * ext[3, upper])
    middle = up_l - lo_r
    hp = 0.5 * vp
    p_l, p_r = flux_weights(roll_left(hp), hp)
    hr = 0.5 * vr
    r_l, r_r = flux_weights(jnp.where(first, hr, roll_below(hr)), hr)
    for c in range(2):
        q = ext[c, row]
        tend = middle * q + (up_r * ext[c, upper] - lo_l * ext[c, lower])
        fp = p_l * roll_left(q) + p_r * q
        fr = r_l * jnp.where(first, q, roll_below(q)) + r_r * q
        tend = tend + (roll_right(fp) - fp)
        tend = tend + (jnp.where(last, q * vr, roll_above(fr)) - fr)
        dout[c, row] = (q - TIME_STEP * tend)[:cols] - dout[c, row]

    scale = TIME_STEP * 0.125
    br, bp = ext[5, row], ext[7, row]
    bp_s = bp + roll_right(bp)
    br_s = br + jnp.where(last, br, roll_above(br))
    vr_bp = vr * bp_s
    e_t = vr_bp - vp * br_s
    e_t0 = vr_bp - vp * (br + br)
    pair = e_t + roll_left(e_t)
    pair0 = e_t0 + roll_left(e_t0)
    edge_t = pair + jnp.where(first, pair0, roll_below(pair))
    new_r = br - scale * (
        (emf[1, row + 2] - emf[1, row]) - (roll_right(edge_t) - edge_t)
    )
    bout[0, row] = new_r[:cols] - bout[0, row]
    edge_t_above = jnp.where(last, 2.0 * pair, roll_above(edge_t))
    new_p = bp - scale * ((edge_t_above - edge_t) - (emf[2, row + 2] - emf[2, row]))
    bout[2, row] = new_p[:cols] - bout[2, row]
    edge_p = emf[1, row] + emf[1, row + 1]
    edge_p_above = jnp.where(last, 2.0 * (emf[0, row] + emf[0, row + 1]), roll_above(edge_p))
    edge_r = emf[2, row] + emf[2, row + 1]
    new_t = ext[6, row] - scale * (
        (roll_right(edge_r) - edge_r) - (edge_p_above - edge_p)
    )
    bout[1, row] = new_t[:cols] - bout[1, row]


def split(x):
    high = x.astype(jnp.bfloat16)
    return high, (x - high.astype(jnp.float32)).astype(jnp.bfloat16)


def product(table, x):
    high, low = split(x)
    dot = functools.partial(jnp.dot, preferred_element_type=jnp.float32)
    return dot(table[0], high) + (dot(table[0], low) + dot(table[1], high))


def kernel(
    n, nt, rows, cols,
    density, velocity, bfield, levels, fwd_hbm, back_hbm,
    dens_hbm, field_hbm,
    ext, dout, bout, out_sem, emf, cyc, part, other_part, fil, gfil, caps, fwd, back, to_right, to_left, at_left, at_right,
    load_sem, fs, fr, ms, mr, rs, rr, gs, gr, g2s, g2r, hs, hr, ts, tr,
):
    half_n = n // 2
    groups = CHANNELS // HUBS * 2
    pole_groups = groups // 2
    wide = cols + 8
    cycle = n * cols
    t = lax.axis_index("theta")
    me = lax.axis_index("phi")
    north = t == 0
    south = t == nt - 1
    end = north | south
    cap0 = jnp.where(north, 0, rows - CAP)
    main = pl.ds(0, cols)
    half = lax.div(me, half_n)
    place = lax.rem(me, half_n)

    def hub_place(j):
        return jnp.where(half == 0, half_n - HUBS + j, j)

    hub_index = place - hub_place(0)
    hub = end & (hub_index >= 0) & (hub_index < HUBS)

    loads = [
        pltpu.make_async_copy(density, ext.at[pl.ds(0, 2), pl.ds(0, rows), main], load_sem.at[0]),
        pltpu.make_async_copy(velocity, ext.at[pl.ds(2, 3), pl.ds(0, rows), main], load_sem.at[1]),
        pltpu.make_async_copy(bfield, ext.at[pl.ds(5, 3), pl.ds(0, rows), main], load_sem.at[2]),
    ]
    width = half_n * wide
    near = pl.ds(pl.multiple_of(half * width, 16), width)
    far = pl.ds(pl.multiple_of((1 - half) * width, 16), width)
    mine = pl.ds(pl.multiple_of(half * half_n * cols, 128), half_n * cols)
    both = pl.ds(0, 2)
    modes = pl.ds(0, 2 * KMAX)
    table_loads = [
        pltpu.make_async_copy(density, dout, load_sem.at[6]),
        pltpu.make_async_copy(bfield, bout, load_sem.at[7]),
        pltpu.make_async_copy(fwd_hbm.at[both, modes, mine], fwd, load_sem.at[3]),
        pltpu.make_async_copy(back_hbm.at[both, near], back.at[0], load_sem.at[4]),
        pltpu.make_async_copy(back_hbm.at[both, far], back.at[1], load_sem.at[5]),
    ]
    for copy in loads + table_loads:
        copy.start()

    barrier = pltpu.get_barrier_semaphore()

    def other(d):
        return lax.rem(me + d, n)

    def greet(device):
        pl.semaphore_signal(barrier, inc=1, device_id=device, device_id_type=MESH)

    right, left = other(1), other(n - 1)

    @pl.when(end)
    def _():
        for d in range(1, n):
            greet({"phi": other(d)})

    @pl.when(jnp.logical_not(end))
    def _():
        greet({"phi": right})
        greet({"phi": left})

    @pl.when(t > 0)
    def _():
        greet({"theta": t - 1})

    @pl.when(t < nt - 1)
    def _():
        greet({"theta": t + 1})

    @pl.when(end)
    def _():
        pl.semaphore_wait(barrier, n)

    @pl.when(jnp.logical_not(end))
    def _():
        pl.semaphore_wait(barrier, 4)

    for copy in loads:
        copy.wait()

    def remote(src, dst, send, recv, device):
        return pltpu.make_async_remote_copy(
            src_ref=src, dst_ref=dst, send_sem=send, recv_sem=recv,
            device_id=device, device_id_type=MESH,
        )

    def await_bytes(ref, sem):
        pltpu.make_async_copy(ref, ref, sem).wait()

    def repeat(count, body):
        def step(i, carry):
            body(i)
            return carry

        lax.fori_loop(0, count, step, 0)

    def cap_pair(g):
        later = lax.div(g, pole_groups)
        return jnp.where(north, CAP - 2 - 2 * later, 2 * later)

    def channel(j, g):
        return j * pole_groups + lax.rem(g, pole_groups)

    def cap_slots(j, g):
        return pl.ds(channel(j, g) * CAP + 2 * lax.div(g, pole_groups), 2)

    def forward_copy(j, g):
        src = ext.at[channel(j, g), pl.ds(cap0 + cap_pair(g), 2), main]
        dst = cyc.at[g, both, pl.ds(pl.multiple_of(place * cols, 8), cols)]
        device = half * half_n + hub_place(j)
        return (
            pltpu.make_async_copy(src, dst, fr.at[g, place]),
            remote(src, dst, fs.at[j, g], fr.at[g, place], {"phi": device}),
        )

    def middle_copy(g):
        partner = jnp.where(half == 0, half_n, half_n - HUBS) + hub_index
        return remote(part.at[g], other_part.at[g], ms.at[g], mr.at[g], {"phi": partner})

    def target(d):
        spot = lax.rem(place + d, half_n)
        return spot, half * half_n + spot

    def return_copy(g, d):
        spot, device = target(d)
        src = fil.at[g, both, spot]
        dst = caps.at[cap_slots(hub_index, g)]
        sem = rr.at[hub_index, g]
        if d == 0:
            return pltpu.make_async_copy(src, dst, sem)
        return remote(src, dst, rs.at[g, d], sem, {"phi": device})

    ghost_row = jnp.where(north, rows + 2, rows)

    def ghost_copy(g, d):
        spot, device = target(d)
        src = gfil.at[g, jnp.where(north, 0, 1), spot]
        dst = ext.at[channel(hub_index, g), ghost_row]
        sem = gr.at[hub_index, g]
        if d == 0:
            return pltpu.make_async_copy(src, dst, sem)
        return remote(src, dst, gs.at[g, d], sem, {"phi": device})

    second_hub, second_group = BTHETA // pole_groups, BTHETA % pole_groups

    def second_copy(d):
        spot, device = target(d)
        src = gfil.at[second_group, 0, spot]
        dst = ext.at[BTHETA, rows + 1]
        if d == 0:
            return pltpu.make_async_copy(src, dst, g2r.at[0])
        return remote(src, dst, g2s.at[d], g2r.at[0], {"phi": device})

    for c in range(CHANNELS):
        to_right[c] = ext[c, 0:rows, cols - 1]
        to_left[c] = ext[c, 0:rows, 0]
    to_left[CHANNELS] = ext[BPHI, 0:rows, 1]

    go_right = remote(to_right, at_left, hs.at[0], hr.at[0], {"phi": right})
    go_left = remote(to_left, at_right, hs.at[1], hr.at[1], {"phi": left})
    go_right.start()
    go_left.start()

    @pl.when(end)
    def _():
        def send(g):
            for j in range(HUBS):
                here, away = forward_copy(j, g)

                @pl.when(hub_place(j) == place)
                def _():
                    here.start()

                @pl.when(hub_place(j) != place)
                def _():
                    away.start()

        repeat(groups, send)

    go_right.wait()
    go_left.wait()

    def unpack(lo, hi):
        for c in range(CHANNELS):
            ext[c, lo:hi, wide - 1] = at_left[c, lo:hi]
            ext[c, lo:hi, cols] = at_right[c, lo:hi]
        ext[BPHI, lo:hi, cols + 1] = at_right[CHANNELS, lo:hi]

    @pl.when(north)
    def _():
        unpack(CAP, rows)

    @pl.when(south)
    def _():
        unpack(0, rows - CAP)

    @pl.when(jnp.logical_not(end))
    def _():
        unpack(0, rows)

    every = pl.ds(0, CHANNELS)
    down = remote(ext.at[every, rows - 1], ext.at[every, rows + 2], ts.at[0], tr.at[0], {"theta": t + 1})
    up = remote(ext.at[every, 0], ext.at[every, rows], ts.at[1], tr.at[1], {"theta": t - 1})
    up2 = remote(ext.at[BTHETA, 1], ext.at[BTHETA, rows + 1], ts.at[2], tr.at[2], {"theta": t - 1})

    @pl.when(t < nt - 1)
    def _():
        down.start()

    @pl.when(t > 0)
    def _():
        up.start()
        up2.start()

    for copy in table_loads:
        copy.wait()

    def row_copies(row):
        return (
            pltpu.make_async_copy(dout.at[pl.ds(0, 2), row], dens_hbm.at[pl.ds(0, 2), row], out_sem.at[0, row]),
            pltpu.make_async_copy(bout.at[pl.ds(0, 3), row], field_hbm.at[pl.ds(0, 3), row], out_sem.at[1, row]),
        )

    def sweep(lo, hi):
        def body(row, carry):
            stencil_row(ext, emf, dout, bout, row, rows, cols)
            for copy in row_copies(row):
                copy.start()
            return carry

        lax.fori_loop(lo, hi, body, 0)

    def make_emfs(lo, hi):
        def body(j, carry):
            emf_row(ext, emf, j, rows, cols)
            return carry

        lax.fori_loop(lo, hi, body, 0)

    early_lo = jnp.where(north, CAP + 1, 0)
    early_hi = jnp.where(south, rows - CAP - 2, rows)

    def ready():
        @pl.when(t > 0)
        def _():
            down.wait_recv()

        @pl.when(t < nt - 1)
        def _():
            up.wait_recv()
            up2.wait_recv()

        make_emfs(jnp.where(north, CAP, -1), jnp.where(south, rows - CAP - 1, rows + 1))

    @pl.when(hub)
    def _():
        pole = jnp.where(north, 0, 1)
        mode = lax.rem(lax.broadcasted_iota(jnp.int32, (2 * KMAX, 128), 0), KMAX)
        weight = jnp.where(mode == 0, 1.0 / cycle, 2.0 / cycle)

        def analyse(g):
            for i in range(half_n):
                await_bytes(cyc.at[g, both, pl.ds(i * cols, cols)], fr.at[g, i])
            part[g] = product(fwd, jnp.concatenate([cyc[g, 0], cyc[g, 1]], axis=1))
            middle_copy(g).start()

        def evaluate(g):
            await_bytes(other_part.at[g], mr.at[g])
            masks = []
            for s in range(2):
                limit = lax.shift_right_logical(jnp.int32(KMAX), levels[pole, cap_pair(g) + s])
                masks.append(jnp.where(mode < limit, weight, 0.0))
            coeffs = (part[g] + other_part[g]) * jnp.concatenate(masks, axis=1)
            values = product(back[0], coeffs)
            fil[g, 0] = values[:, :128].reshape(half_n, wide, 128)
            fil[g, 1] = values[:, 128:].reshape(half_n, wide, 128)
            for d in reversed(range(half_n)):
                return_copy(g, d).start()

            @pl.when(g >= pole_groups)
            def _():
                k = g - pole_groups
                ghosts = product(back[1], coeffs)
                gfil[k, 0] = ghosts[:, :128].reshape(half_n, wide, 128)
                gfil[k, 1] = ghosts[:, 128:].reshape(half_n, wide, 128)
                for d in reversed(range(half_n)):
                    ghost_copy(k, d).start()

        repeat(groups, analyse)
        ready()

        def step(g):
            row = early_lo + g
            sweep(row, jnp.minimum(row + 1, early_hi))
            evaluate(g)

        repeat(groups, step)
        sweep(early_lo + groups, early_hi)

    @pl.when(south & hub & (hub_index == second_hub))
    def _():
        for d in range(half_n):
            second_copy(d).start()

    @pl.when(jnp.logical_not(hub))
    def _():
        ready()
        sweep(early_lo, early_hi)

    @pl.when(end)
    def _():
        def sent(g):
            for j in range(HUBS):
                @pl.when(hub_place(j) != place)
                def _():
                    forward_copy(j, g)[1].wait_send()

        repeat(groups, sent)

        def take(first):
            def one(k):
                g = first + k
                for j in range(HUBS):
                    slots = cap_slots(j, g)
                    await_bytes(caps.at[slots], rr.at[j, g])
                    c = channel(j, g)
                    slot = c * CAP + 2 * lax.div(g, pole_groups)
                    r = cap0 + cap_pair(g)
                    ext[c, r] = caps[slot]
                    ext[c, r + 1] = caps[slot + 1]

            repeat(pole_groups, one)

        take(0)
        make_emfs(
            jnp.where(north, CAP - 2, rows - CAP - 1), jnp.where(north, CAP, rows - CAP + 1)
        )
        sweep(jnp.where(north, CAP - 1, rows - CAP - 2), jnp.where(north, CAP + 1, rows - CAP))
        take(pole_groups)

        def ghost(k):
            for j in range(HUBS):
                await_bytes(ext.at[channel(j, k), ghost_row], gr.at[j, k])

        repeat(pole_groups, ghost)
        for c in ODD:
            ext[c, ghost_row] = -ext[c, ghost_row]

        @pl.when(south)
        def _():
            await_bytes(ext.at[BTHETA, rows + 1], g2r.at[0])
            ext[BTHETA, rows + 1] = -ext[BTHETA, rows + 1]

        make_emfs(jnp.where(north, -1, rows - CAP + 1), jnp.where(north, CAP - 2, rows + 1))
        sweep(jnp.where(north, 0, rows - CAP), jnp.where(north, CAP - 1, rows))

    def wait_row(row):
        for copy in row_copies(row):
            copy.wait()

    repeat(rows, wait_row)

    @pl.when(t < nt - 1)
    def _():
        down.wait_send()

    @pl.when(t > 0)
    def _():
        up.wait_send()
        up2.wait_send()

    @pl.when(hub)
    def _():
        def drain(g):
            middle_copy(g).wait_send()
            for d in range(1, half_n):
                return_copy(g, d).wait_send()

        def drain_ghost(g):
            for d in range(1, half_n):
                ghost_copy(g, d).wait_send()

        repeat(groups, drain)
        repeat(pole_groups, drain_ghost)

    @pl.when(south & hub & (hub_index == second_hub))
    def _():
        for d in range(1, half_n):
            second_copy(d).wait_send()


def local(n, nt, density, velocity, bfield, levels):
    _, rows, cols, radial = density.shape
    half_n = n // 2
    groups = CHANNELS // HUBS * 2
    wide = cols + 8
    forward, back = tables(n, cols)
    any_space = pl.BlockSpec(memory_space=pl.ANY)
    f32, bf16 = jnp.float32, jnp.bfloat16
    dma = pltpu.SemaphoreType.DMA
    density_change, field_change = pl.pallas_call(
        functools.partial(kernel, n, nt, rows, cols),
        out_shape=(
            jax.ShapeDtypeStruct(density.shape, f32),
            jax.ShapeDtypeStruct(bfield.shape, f32),
        ),
        in_specs=[any_space] * 3 + [pl.BlockSpec(memory_space=pltpu.SMEM)] + [any_space] * 2,
        out_specs=(any_space, any_space),
        scratch_shapes=[
            pltpu.VMEM((CHANNELS, rows + 3, wide, radial), f32),
            pltpu.VMEM(density.shape, f32),
            pltpu.VMEM(bfield.shape, f32),
            dma((2, rows)),
            pltpu.VMEM((3, rows + 2, wide, radial), f32),
            pltpu.VMEM((groups, 2, half_n * cols, radial), f32),
            pltpu.VMEM((groups, 2 * KMAX, 2 * radial), f32),
            pltpu.VMEM((groups, 2 * KMAX, 2 * radial), f32),
            pltpu.VMEM((groups, 2, half_n, wide, radial), f32),
            pltpu.VMEM((groups // 2, 2, half_n, wide, radial), f32),
            pltpu.VMEM((CHANNELS * CAP, wide, radial), f32),
            pltpu.VMEM((2, 2 * KMAX, half_n * cols), bf16),
            pltpu.VMEM((2, 2, half_n * wide, 2 * KMAX), bf16),
            pltpu.VMEM((CHANNELS, rows, radial), f32),
            pltpu.VMEM((CHANNELS + 1, rows, radial), f32),
            pltpu.VMEM((CHANNELS, rows, radial), f32),
            pltpu.VMEM((CHANNELS + 1, rows, radial), f32),
            dma((8,)),
            dma((HUBS, groups)),
            dma((groups, half_n)),
            dma((groups,)),
            dma((groups,)),
            dma((groups, half_n)),
            dma((HUBS, groups)),
            dma((groups // 2, half_n)),
            dma((HUBS, groups // 2)),
            dma((half_n,)),
            dma((1,)),
            dma((2,)),
            dma((2,)),
            dma((3,)),
            dma((3,)),
        ],
        compiler_params=pltpu.CompilerParams(
            collective_id=0, has_side_effects=True, vmem_limit_bytes=56 * 1024 * 1024
        ),
        name="substep",
    )(density, velocity, bfield, levels, jnp.asarray(forward), jnp.asarray(back))
    return density + density_change, bfield + field_change


def solution(mesh):
    spec = P(None, "theta", "phi", None)
    return jax.shard_map(
        functools.partial(local, mesh.shape["phi"], mesh.shape["theta"]),
        mesh=mesh,
        in_specs=(spec, spec, spec, P()),
        out_specs=(spec, spec),
        check_vma=False,
    )
```
